512 devices in a mesh: row: 32 (over x, y, core), col: 16 (over z).
Axes of the slice: x: 4, y: 4, z: 16, core: 2. Of those that a mesh axis runs over, the one named last changes fastest.
Arguments:
- matrix: float32 [12800, 12800], P('row', 'col'), may hold values from -1.1 to 1.2, as said below
Outputs:
- swept: float32 [12800, 12800], P('row', 'col')
The draws below stay inside these ranges and needn't reach their ends.
Inputs may be any that keep to these rules, and one draw needn't show every extreme that they name: `matrix`: exactly symmetric and positive definite.
All inputs are finite; a program needn't handle non-finite values.
Results may differ from the reference program's by a relative error of at most 0.00018.
Values sent between devices are 32-bit elements; how exact they have to be, the bound alone decides.
No kernel may reach another device: no remote copies, remote signals or barrier semaphores. Data moves between devices by JAX's collectives and lax.ppermute only.
A program may use at most 64 MiB of HBM per device.

```python
import jax
import jax.numpy as jnp
from jax import lax

M = 12800
Q = 20
B = 384
K = 2
N_ROW = 32


def mutate_states(key, parent, per_mille):
    first, second = jax.random.split(key)
    mutated = jax.random.randint(first, parent.shape, 0, 1000) < per_mille
    fresh_state = jax.random.randint(second, parent.shape, 0, Q + 1)
    return jnp.where(mutated, fresh_state, parent)


def potts_correlation(key, mixing, ridge_term):
    seq_count = 1024
    positions = M // Q
    streams = jax.random.split(key, 6)
    root_state = jax.random.randint(streams[0], (1, positions), 0, Q)
    level_one = mutate_states(streams[1], root_state[jnp.zeros((4,), jnp.int32)], 250)
    level_two = mutate_states(streams[2], level_one[jnp.arange(16, dtype=jnp.int32) // 4], 200)
    level_three = mutate_states(streams[3], level_two[jnp.arange(64, dtype=jnp.int32) // 4], 150)
    leaves = jax.random.randint(streams[4], (seq_count,), 0, 64)
    sequences = mutate_states(streams[5], level_three[leaves], 100)
    onehot = (sequences[:, :, None] == jnp.arange(Q, dtype=jnp.int32)[None, None, :]).astype(jnp.float32).reshape(seq_count, M)
    counts = jnp.dot(onehot.T, onehot, precision=lax.Precision.HIGHEST)
    frequency = jnp.diagonal(counts) / seq_count
    position = jnp.arange(M, dtype=jnp.int32) // Q
    same_position = position[:, None] == position[None, :]
    diagonal_mask = jnp.arange(M, dtype=jnp.int32)[:, None] == jnp.arange(M, dtype=jnp.int32)[None, :]
    uniform_pair = jnp.where(same_position, jnp.where(diagonal_mask, 1.0 / (Q + 1), 0.0), 1.0 / ((Q + 1) * (Q + 1)))
    single = (1.0 - mixing) * frequency + mixing / (Q + 1)
    pair_freq = (1.0 - mixing) * (counts / seq_count) + mixing * uniform_pair
    covariance = pair_freq - single[:, None] * single[None, :]
    return (4.0 * covariance + jnp.where(diagonal_mask, ridge_term, 0.0)).astype(jnp.float32)


def draw_matrix(key, part):
    key = jax.random.fold_in(key, 11)
    mixing = 0.5
    ridge_term = 0.1
    return potts_correlation(key, mixing, ridge_term)


def setup_inputs(seed: int = 0) -> dict:
    key_list = jax.random.split(jax.random.key(seed), 2)
    return {
        "matrix": draw_matrix(jax.random.fold_in(key_list[1], 71), 0),
    }


def cholesky_solve(factor_low, right_side):
    middle = lax.linalg.triangular_solve(factor_low, right_side, left_side=True, lower=True)
    return lax.linalg.triangular_solve(factor_low, middle, left_side=True, lower=True, transpose_a=True)

def sweep_step(current, step_index):
    local_rows = M // N_ROW
    piece_rows = B // N_ROW
    indices = (jnp.arange(N_ROW, dtype=jnp.int32)[:, None] * local_rows + step_index * piece_rows + jnp.arange(piece_rows, dtype=jnp.int32)[None, :]).reshape(-1).astype(jnp.int32)
    colpanel = current[:, indices]
    rowpanel = current[indices, :]
    pivot_block = rowpanel[:, indices]
    factor_low = jnp.linalg.cholesky(pivot_block)
    inverse = cholesky_solve(factor_low, jnp.eye(B, dtype=current.dtype))
    scaled = cholesky_solve(factor_low, colpanel.T).T
    lifted = jnp.dot(inverse, rowpanel, precision=lax.Precision.HIGHEST)
    updated = current - jnp.dot(scaled, rowpanel, precision=lax.Precision.HIGHEST)
    updated = updated.at[indices, :].set(lifted)
    updated = updated.at[:, indices].set(scaled)
    updated = updated.at[indices[:, None], indices[None, :]].set(-inverse)
    return updated

def reference(matrix):
    current = matrix
    for step_index in range(K):
        current = sweep_step(current, step_index)
    return current
```

```python
import functools

import jax
import jax.numpy as jnp
from jax import lax
from jax.experimental import pallas as pl
from jax.experimental.pallas import tpu as pltpu
from jax.sharding import Mesh
from jax.sharding import PartitionSpec as P

B = 384
K = 2
F32 = jnp.float32
HIGHEST = lax.Precision.HIGHEST
TILE = 128


def lane_splat(tile, lane):
    return jnp.broadcast_to(tile[:, lane : lane + 1], (8, TILE))


def row_splat(tile, row):
    return jnp.broadcast_to(tile[row : row + 1, :], (8, TILE))


def solve_eight(pivot, right):
    size = 8
    pivot = [list(row) for row in pivot]
    right = list(right)
    factor = [[None] * size for _ in range(size)]
    scale = [None] * size
    for j in range(size):
        recip = 1.0 / pivot[j][j]
        scale[j] = recip
        for m in range(j + 1, size):
            factor[m][j] = pivot[m][j] * recip
        for m in range(j + 1, size):
            for q in range(j + 1, m + 1):
                pivot[m][q] = pivot[m][q] - (pivot[m][j] * pivot[q][j]) * recip
            right[m] = right[m] - factor[m][j] * right[j]
    for j in range(size):
        right[j] = right[j] * scale[j]
    for j in reversed(range(size)):
        for m in range(j):
            right[m] = right[m] - factor[j][m] * right[j]
    return right


def invert_tile(rows):
    lane = lax.broadcasted_iota(jnp.int32, (8, TILE), 1)
    sub = lax.broadcasted_iota(jnp.int32, (8, TILE), 0)
    groups = len(rows)
    rows = list(rows)
    for g in range(groups):
        first = 8 * g
        here = rows[g]
        inside = (lane >= first) & (lane < first + 8)
        columns = [lane_splat(here, first + j) for j in range(8)]
        pivot = [[row_splat(columns[j], i) for j in range(i + 1)] for i in range(8)]
        start = jnp.where(inside, jnp.where(lane == first + sub, 1.0, 0.0), here)
        solved = solve_eight(pivot, [row_splat(start, i) for i in range(8)])
        for step in range(1, groups):
            i = (g + step) % groups
            terms = [lane_splat(rows[i], first + j) * solved[j] for j in range(8)]
            while len(terms) > 1:
                terms = [terms[2 * q] + terms[2 * q + 1] for q in range(len(terms) // 2)]
            rows[i] = jnp.where(inside, 0.0, rows[i]) - terms[0]
        merged = solved[0]
        for j in range(1, 8):
            merged = jnp.where(sub == j, solved[j], merged)
        rows[g] = merged
    return rows


def inverse_kernel(core_ref, own_ref, other_ref, out_ref):
    pairs, band, order = own_ref.shape
    core = core_ref[0]
    for i in range(pairs):
        out_ref[pl.ds(pl.multiple_of((2 * i + core) * band, 8), band), :] = own_ref[i]
        out_ref[pl.ds(pl.multiple_of((2 * i + 1 - core) * band, 8), band), :] = other_ref[i]
    unit = lax.broadcasted_iota(jnp.int32, (TILE, TILE), 0) == lax.broadcasted_iota(
        jnp.int32, (TILE, TILE), 1
    )

    def step(k, carry):
        here = pl.ds(pl.multiple_of(k * TILE, TILE), TILE)
        rows = invert_tile([out_ref[here, here][8 * i : 8 * i + 8, :] for i in range(TILE // 8)])
        inverse = jnp.concatenate(rows, axis=0)
        column = out_ref[:, here]
        out_ref[:, here] = jnp.zeros((order, TILE), F32)
        out_ref[here, here] = jnp.where(unit, 1.0, 0.0)
        lifted = jnp.dot(inverse, out_ref[here, :], precision=HIGHEST, preferred_element_type=F32)
        out_ref[here, here] = jnp.zeros((TILE, TILE), F32)
        out_ref[...] = out_ref[...] - jnp.dot(
            column, lifted, precision=HIGHEST, preferred_element_type=F32
        )
        out_ref[here, :] = lifted
        return carry

    lax.fori_loop(0, order // TILE, step, 0)


def pivot_inverse(core, own, other):
    order = own.shape[2]
    vmem = pl.BlockSpec(memory_space=pltpu.VMEM)
    return pl.pallas_call(
        inverse_kernel,
        out_shape=jax.ShapeDtypeStruct((order, order), F32),
        in_specs=[pl.BlockSpec(memory_space=pltpu.SMEM), vmem, vmem],
        out_specs=vmem,
        compiler_params=pltpu.CompilerParams(vmem_limit_bytes=20 * 1024 * 1024),
        cost_estimate=pl.CostEstimate(
            flops=order, bytes_accessed=8 * order, transcendentals=0
        ),
        name="pivot_inverse",
    )(core, own, other)


def update_kernel(place_ref, current_ref, column_ref, row_ref, inverse_ref, out_ref, *, band):
    rows, cols = current_ref.shape
    order = inverse_ref.shape[0]
    span = rows
    my_rows = place_ref[0] * band
    my_cols = place_ref[1] * (cols // span) * band

    def iota(shape, axis):
        return lax.broadcasted_iota(jnp.int32, shape, axis)

    column = column_ref[...]
    shape = (rows, order)
    pick = jnp.where(iota(shape, 1) == iota(shape, 0) + my_rows, -1.0, 0.0)
    column = jnp.where(iota(shape, 0) < band, pick, column)
    scaled = jnp.dot(column, inverse_ref[...], precision=HIGHEST, preferred_element_type=F32)

    def strip_of(shape):
        at = iota(shape, 1)
        inside = at < band
        within = at
        for g in range(1, cols // span):
            past = at - g * span
            now = (past >= 0) & (past < band)
            inside = inside | now
            within = jnp.where(now, past + g * band, within)
        return inside, within

    shape = (order, cols)
    inside, within = strip_of(shape)
    pick = jnp.where(iota(shape, 0) == within + my_cols, -1.0, 0.0)
    row = jnp.where(inside, pick, row_ref[...])
    shape = (rows, cols)
    inside, _ = strip_of(shape)
    base = jnp.where(inside | (iota(shape, 0) < band), 0.0, current_ref[...])
    out_ref[...] = base - jnp.dot(scaled, row, precision=HIGHEST, preferred_element_type=F32)


def trailing_update(place, current, column, row, inverse, band):
    vmem = pl.BlockSpec(memory_space=pltpu.VMEM)
    rows, cols = current.shape
    order = inverse.shape[0]
    return pl.pallas_call(
        functools.partial(update_kernel, band=band),
        out_shape=jax.ShapeDtypeStruct(current.shape, F32),
        in_specs=[pl.BlockSpec(memory_space=pltpu.SMEM)] + [vmem] * 4,
        out_specs=vmem,
        compiler_params=pltpu.CompilerParams(vmem_limit_bytes=20 * 1024 * 1024),
        cost_estimate=pl.CostEstimate(
            flops=2 * rows * order * (cols + order), bytes_accessed=8 * rows * cols, transcendentals=0
        ),
        name="trailing_update",
    )(place, current, column, row, inverse)


def body(matrix):
    rows, cols = matrix.shape
    groups = cols // rows
    depth = lax.axis_size("z")
    chips = lax.axis_size("x") * lax.axis_size("y")
    band = K * B // (2 * chips)
    core = lax.axis_index("c")
    place = jnp.stack([lax.axis_index(("x", "y", "c")), lax.axis_index("z")]).astype(jnp.int32)
    strip = jnp.concatenate(
        [matrix[:, g * rows : g * rows + band] for g in range(groups)], axis=1
    )
    rowband = matrix[0:band, :]
    with jax.named_scope("pivot_z"):
        pivot = lax.all_to_all(
            jnp.broadcast_to(strip[0:band, :], (depth, band, groups * band)), "z", 0, 0
        )
    pivot = pivot.transpose(1, 0, 2).reshape(band, K * B)
    with jax.named_scope("pivot_xy"):
        own = lax.all_to_all(jnp.broadcast_to(pivot, (chips, band, K * B)), ("x", "y"), 0, 0)
    with jax.named_scope("pivot_core"):
        other = lax.ppermute(own, "c", [(0, 1), (1, 0)])
    with jax.named_scope("column_panel"):
        column = lax.all_gather(strip.T, "z", axis=0, tiled=True)
    rowband = lax.optimization_barrier((rowband, own))[0]
    with jax.named_scope("row_panel"):
        row = lax.all_to_all(
            jnp.broadcast_to(rowband, (2 * chips, band, cols)), ("x", "y", "c"), 0, 0
        )
    inverse = pivot_inverse(core.astype(jnp.int32)[None], own, other)
    column, row, inverse = lax.optimization_barrier((column, row, inverse))
    return trailing_update(
        place, matrix, column.T, row.reshape(K * B, cols), inverse, band
    )


def solution(mesh):
    split = Mesh(mesh.devices.reshape(4, 4, 2, 16), ("x", "y", "c", "z"))
    spec = P(("x", "y", "c"), "z")
    return jax.shard_map(body, mesh=split, in_specs=(spec,), out_specs=spec, check_vma=False)
```

```python
import functools

import jax
import jax.numpy as jnp
from jax import lax
from jax.experimental import pallas as pl
from jax.experimental.pallas import tpu as pltpu
from jax.sharding import Mesh
from jax.sharding import PartitionSpec as P

B = 384
K = 2
F32 = jnp.float32
BF16 = jnp.bfloat16
HIGHEST = lax.Precision.HIGHEST
TILE = 128


def lane_splat(tile, lane):
    return jnp.broadcast_to(tile[:, lane : lane + 1], (8, TILE))


def row_splat(tile, row):
    return jnp.broadcast_to(tile[row : row + 1, :], (8, TILE))


def solve_eight(pivot, right):
    size = 8
    pivot = [list(row) for row in pivot]
    right = list(right)
    factor = [[None] * size for _ in range(size)]
    scale = [None] * size
    for j in range(size):
        recip = 1.0 / pivot[j][j]
        scale[j] = recip
        for m in range(j + 1, size):
            factor[m][j] = pivot[m][j] * recip
        for m in range(j + 1, size):
            for q in range(j + 1, m + 1):
                pivot[m][q] = pivot[m][q] - (pivot[m][j] * pivot[q][j]) * recip
            right[m] = right[m] - factor[m][j] * right[j]
    for j in range(size):
        right[j] = right[j] * scale[j]
    for j in reversed(range(size)):
        for m in range(j):
            right[m] = right[m] - factor[j][m] * right[j]
    return right


def invert_tile(rows):
    lane = lax.broadcasted_iota(jnp.int32, (8, TILE), 1)
    sub = lax.broadcasted_iota(jnp.int32, (8, TILE), 0)
    groups = len(rows)
    rows = list(rows)
    for g in range(groups):
        first = 8 * g
        here = rows[g]
        inside = (lane >= first) & (lane < first + 8)
        columns = [lane_splat(here, first + j) for j in range(8)]
        pivot = [[row_splat(columns[j], i) for j in range(i + 1)] for i in range(8)]
        start = jnp.where(inside, jnp.where(lane == first + sub, 1.0, 0.0), here)
        solved = solve_eight(pivot, [row_splat(start, i) for i in range(8)])
        for step in range(1, groups):
            i = (g + step) % groups
            terms = [lane_splat(rows[i], first + j) * solved[j] for j in range(8)]
            while len(terms) > 1:
                terms = [terms[2 * q] + terms[2 * q + 1] for q in range(len(terms) // 2)]
            rows[i] = jnp.where(inside, 0.0, rows[i]) - terms[0]
        merged = solved[0]
        for j in range(1, 8):
            merged = jnp.where(sub == j, solved[j], merged)
        rows[g] = merged
    return rows


def three_parts(value):
    high = value.astype(BF16)
    rest = value - high.astype(F32)
    middle = rest.astype(BF16)
    return high, middle, (rest - middle.astype(F32)).astype(BF16)


def left_parts(value):
    high, middle, low = three_parts(value)
    return jnp.concatenate([high, high, middle, high, low, middle], axis=1)


def right_parts(value):
    high, middle, low = three_parts(value)
    return jnp.concatenate([high, middle, high, low, high, middle], axis=0)


def product(left, right):
    return jnp.dot(left, right, preferred_element_type=F32)


def inverse_kernel(core_ref, own_ref, other_ref, out_ref, left_ref, right_ref, diagonal_ref):
    pairs, band, order = own_ref.shape
    blocks = order // TILE
    core = core_ref[0]
    for i in range(pairs):
        out_ref[pl.ds(pl.multiple_of((2 * i + core) * band, 8), band), :] = own_ref[i]
        out_ref[pl.ds(pl.multiple_of((2 * i + 1 - core) * band, 8), band), :] = other_ref[i]
    unit = lax.broadcasted_iota(jnp.int32, (TILE, TILE), 0) == lax.broadcasted_iota(
        jnp.int32, (TILE, TILE), 1
    )
    unit = jnp.where(unit, 1.0, 0.0)
    diagonal_ref[...] = out_ref[0:TILE, 0:TILE]
    left_ref[...] = jnp.zeros(left_ref.shape, BF16)
    right_ref[...] = jnp.zeros(right_ref.shape, BF16)

    def apply_last():
        for c in range(blocks):
            here = slice(TILE * c, TILE * c + TILE)
            out_ref[:, here] = out_ref[:, here] - product(left_ref[...], right_ref[:, here])

    def step(k, carry):
        here = pl.ds(pl.multiple_of(k * TILE, TILE), TILE)
        apply_last()
        block = diagonal_ref[...]
        rows = invert_tile([block[8 * i : 8 * i + 8, :] for i in range(TILE // 8)])
        inverse = jnp.concatenate(rows, axis=0)
        row = out_ref[here, :]
        out_ref[here, here] = -unit
        column = out_ref[:, here]
        out_ref[:, here] = jnp.zeros((order, TILE), F32)
        left_ref[...] = left_parts(product(left_parts(column), right_parts(inverse)))
        right_ref[...] = right_parts(row)
        right_ref[:, here] = right_parts(unit)
        out_ref[here, :] = jnp.zeros((TILE, order), F32)
        after = pl.ds(pl.multiple_of(jnp.minimum(k + 1, blocks - 1) * TILE, TILE), TILE)
        diagonal_ref[...] = out_ref[after, after] - product(left_ref[after, :], right_ref[:, after])
        return carry

    lax.fori_loop(0, blocks, step, 0)
    apply_last()


def pivot_inverse(core, own, other):
    order = own.shape[2]
    vmem = pl.BlockSpec(memory_space=pltpu.VMEM)
    return pl.pallas_call(
        inverse_kernel,
        out_shape=jax.ShapeDtypeStruct((order, order), F32),
        in_specs=[pl.BlockSpec(memory_space=pltpu.SMEM), vmem, vmem],
        out_specs=vmem,
        scratch_shapes=[
            pltpu.VMEM((order, 6 * TILE), BF16),
            pltpu.VMEM((6 * TILE, order), BF16),
            pltpu.VMEM((TILE, TILE), F32),
        ],
        compiler_params=pltpu.CompilerParams(vmem_limit_bytes=20 * 1024 * 1024),
        cost_estimate=pl.CostEstimate(flops=1, bytes_accessed=8, transcendentals=0),
        name="pivot_inverse",
    )(core, own, other)


def update_kernel(place_ref, column_ref, row_ref, inverse_ref, current_ref, out_ref, held, sem, *, band):
    copy = pltpu.make_async_copy(current_ref, held, sem)
    copy.start()
    rows, cols = held.shape
    order = inverse_ref.shape[0]
    span = rows
    my_rows = place_ref[0] * band
    my_cols = place_ref[1] * (cols // span) * band

    def iota(shape, axis):
        return lax.broadcasted_iota(jnp.int32, shape, axis)

    shape = (order, rows)
    pick = jnp.where(iota(shape, 0) == iota(shape, 1) + my_rows, -1.0, 0.0)
    column = jnp.where(iota(shape, 1) < band, pick, column_ref[...])
    scaled = jnp.dot(inverse_ref[...], column, precision=HIGHEST, preferred_element_type=F32).T

    def strip_of(shape):
        at = iota(shape, 1)
        inside = at < band
        within = at
        for g in range(1, cols // span):
            past = at - g * span
            now = (past >= 0) & (past < band)
            inside = inside | now
            within = jnp.where(now, past + g * band, within)
        return inside, within

    shape = (order, cols)
    inside, within = strip_of(shape)
    pick = jnp.where(iota(shape, 0) == within + my_cols, -1.0, 0.0)
    row = jnp.where(inside, pick, row_ref[...])
    shape = (rows, cols)
    inside, _ = strip_of(shape)
    scaled_high, scaled_low, _ = three_parts(scaled)
    row_high, row_low, _ = three_parts(row)
    change = product(scaled_high, row_high) + (
        product(scaled_high, row_low) + product(scaled_low, row_high)
    )
    copy.wait()
    base = jnp.where(inside | (iota(shape, 0) < band), 0.0, held[...])
    out_ref[...] = base - change


def trailing_update(place, current, column, row, inverse, band):
    vmem = pl.BlockSpec(memory_space=pltpu.VMEM)
    rows, cols = current.shape
    order = inverse.shape[0]
    return pl.pallas_call(
        functools.partial(update_kernel, band=band),
        out_shape=jax.ShapeDtypeStruct(current.shape, F32),
        in_specs=[pl.BlockSpec(memory_space=pltpu.SMEM)]
        + [vmem] * 3
        + [pl.BlockSpec(memory_space=pl.ANY)],
        out_specs=vmem,
        scratch_shapes=[pltpu.VMEM(current.shape, F32), pltpu.SemaphoreType.DMA(())],
        compiler_params=pltpu.CompilerParams(vmem_limit_bytes=20 * 1024 * 1024),
        cost_estimate=pl.CostEstimate(
            flops=2 * rows * order * (cols + order), bytes_accessed=8 * rows * cols, transcendentals=0
        ),
        name="trailing_update",
    )(place, column, row, inverse, current)


def body(matrix):
    rows, cols = matrix.shape
    groups = cols // rows
    depth = lax.axis_size("z")
    chips = lax.axis_size("x") * lax.axis_size("y")
    band = K * B // (2 * chips)
    core = lax.axis_index("c")
    place = jnp.stack([lax.axis_index(("x", "y", "c")), lax.axis_index("z")]).astype(jnp.int32)
    strip = jnp.concatenate(
        [matrix[:, g * rows : g * rows + band] for g in range(groups)], axis=1
    )
    rowband = matrix[0:band, :]
    with jax.named_scope("pivot_z"):
        pivot = lax.all_to_all(
            jnp.broadcast_to(strip[0:band, :], (depth, band, groups * band)), "z", 0, 0
        )
    pivot = pivot.transpose(1, 0, 2).reshape(band, K * B)
    with jax.named_scope("pivot_xy"):
        own = lax.all_to_all(jnp.broadcast_to(pivot, (chips, band, K * B)), ("x", "y"), 0, 0)
    with jax.named_scope("pivot_core"):
        other = lax.ppermute(own, "c", [(0, 1), (1, 0)])
    with jax.named_scope("column_panel"):
        column = lax.all_gather(strip.T, "z", axis=0, tiled=True)
    with jax.named_scope("row_panel"):
        row = lax.all_gather(rowband, ("x", "y", "c"), axis=0, tiled=True)
    inverse = pivot_inverse(core.astype(jnp.int32)[None], own, other)
    column, row, inverse = lax.optimization_barrier((column, row, inverse))
    return trailing_update(
        place, matrix, column, row.reshape(K * B, cols), inverse, band
    )


def solution(mesh):
    split = Mesh(mesh.devices.reshape(4, 4, 2, 16), ("x", "y", "c", "z"))
    spec = P(("x", "y", "c"), "z")
    return jax.shard_map(body, mesh=split, in_specs=(spec,), out_specs=spec, check_vma=False)
```

```python
import functools

import jax
import jax.numpy as jnp
from jax import lax
from jax.experimental import pallas as pl
from jax.experimental.pallas import tpu as pltpu
from jax.sharding import Mesh
from jax.sharding import PartitionSpec as P

B = 384
K = 2
F32 = jnp.float32
BF16 = jnp.bfloat16
HIGHEST = lax.Precision.HIGHEST
TILE = 128


def lane_splat(tile, lane):
    return jnp.broadcast_to(tile[:, lane : lane + 1], (8, TILE))


def row_splat(tile, row):
    return jnp.broadcast_to(tile[row : row + 1, :], (8, TILE))


def solve_eight(pivot, right):
    size = 8
    pivot = [list(row) for row in pivot]
    right = list(right)
    factor = [[None] * size for _ in range(size)]
    scale = [None] * size
    for j in range(size):
        recip = 1.0 / pivot[j][j]
        scale[j] = recip
        for m in range(j + 1, size):
            factor[m][j] = pivot[m][j] * recip
        for m in range(j + 1, size):
            for q in range(j + 1, m + 1):
                pivot[m][q] = pivot[m][q] - (pivot[m][j] * pivot[q][j]) * recip
            right[m] = right[m] - factor[m][j] * right[j]
    for j in range(size):
        right[j] = right[j] * scale[j]
    for j in reversed(range(size)):
        for m in range(j):
            right[m] = right[m] - factor[j][m] * right[j]
    return right


def invert_tile(rows):
    lane = lax.broadcasted_iota(jnp.int32, (8, TILE), 1)
    sub = lax.broadcasted_iota(jnp.int32, (8, TILE), 0)
    groups = len(rows)
    rows = list(rows)
    for g in range(groups):
        first = 8 * g
        here = rows[g]
        inside = (lane >= first) & (lane < first + 8)
        columns = [lane_splat(here, first + j) for j in range(8)]
        pivot = [[row_splat(columns[j], i) for j in range(i + 1)] for i in range(8)]
        start = jnp.where(inside, jnp.where(lane == first + sub, 1.0, 0.0), here)
        solved = solve_eight(pivot, [row_splat(start, i) for i in range(8)])
        for step in range(1, groups):
            i = (g + step) % groups
            terms = [lane_splat(rows[i], first + j) * solved[j] for j in range(8)]
            while len(terms) > 1:
                terms = [terms[2 * q] + terms[2 * q + 1] for q in range(len(terms) // 2)]
            rows[i] = jnp.where(inside, 0.0, rows[i]) - terms[0]
        merged = solved[0]
        for j in range(1, 8):
            merged = jnp.where(sub == j, solved[j], merged)
        rows[g] = merged
    return rows


def three_parts(value):
    high = value.astype(BF16)
    rest = value - high.astype(F32)
    middle = rest.astype(BF16)
    return high, middle, (rest - middle.astype(F32)).astype(BF16)


def left_parts(value):
    high, middle, low = three_parts(value)
    return jnp.concatenate([high, high, middle, high, low, middle], axis=1)


def right_parts(value):
    high, middle, low = three_parts(value)
    return jnp.concatenate([high, middle, high, low, high, middle], axis=0)


def product(left, right):
    return jnp.dot(left, right, preferred_element_type=F32)


def inverse_kernel(slot_ref, own_ref, other_ref, out_ref, left_ref, right_ref, diagonal_ref):
    pairs, band, order = own_ref.shape
    blocks = order // TILE
    for i in range(pairs):
        out_ref[pl.ds(pl.multiple_of(slot_ref[0, i] * band, 8), band), :] = own_ref[i]
        out_ref[pl.ds(pl.multiple_of(slot_ref[1, i] * band, 8), band), :] = other_ref[i]
    unit = lax.broadcasted_iota(jnp.int32, (TILE, TILE), 0) == lax.broadcasted_iota(
        jnp.int32, (TILE, TILE), 1
    )
    unit = jnp.where(unit, 1.0, 0.0)
    diagonal_ref[...] = out_ref[0:TILE, 0:TILE]
    left_ref[...] = jnp.zeros(left_ref.shape, BF16)
    right_ref[...] = jnp.zeros(right_ref.shape, BF16)

    def apply_last():
        for c in range(blocks):
            here = slice(TILE * c, TILE * c + TILE)
            out_ref[:, here] = out_ref[:, here] - product(left_ref[...], right_ref[:, here])

    def step(k, carry):
        here = pl.ds(pl.multiple_of(k * TILE, TILE), TILE)
        apply_last()
        block = diagonal_ref[...]
        rows = invert_tile([block[8 * i : 8 * i + 8, :] for i in range(TILE // 8)])
        inverse = jnp.concatenate(rows, axis=0)
        row = out_ref[here, :]
        out_ref[here, here] = -unit
        column = out_ref[:, here]
        out_ref[:, here] = jnp.zeros((order, TILE), F32)
        left_ref[...] = left_parts(product(left_parts(column), right_parts(inverse)))
        right_ref[...] = right_parts(row)
        right_ref[:, here] = right_parts(unit)
        out_ref[here, :] = jnp.zeros((TILE, order), F32)
        after = pl.ds(pl.multiple_of(jnp.minimum(k + 1, blocks - 1) * TILE, TILE), TILE)
        diagonal_ref[...] = out_ref[after, after] - product(left_ref[after, :], right_ref[:, after])
        return carry

    lax.fori_loop(0, blocks, step, 0)
    apply_last()


def pivot_inverse(slots, own, other):
    order = own.shape[2]
    vmem = pl.BlockSpec(memory_space=pltpu.VMEM)
    return pl.pallas_call(
        inverse_kernel,
        out_shape=jax.ShapeDtypeStruct((order, order), F32),
        in_specs=[pl.BlockSpec(memory_space=pltpu.SMEM), vmem, vmem],
        out_specs=vmem,
        scratch_shapes=[
            pltpu.VMEM((order, 6 * TILE), BF16),
            pltpu.VMEM((6 * TILE, order), BF16),
            pltpu.VMEM((TILE, TILE), F32),
        ],
        compiler_params=pltpu.CompilerParams(vmem_limit_bytes=20 * 1024 * 1024),
        cost_estimate=pl.CostEstimate(flops=1, bytes_accessed=8, transcendentals=0),
        name="pivot_inverse",
    )(slots, own, other)


def update_kernel(
    place_ref, column_hbm, inverse_hbm, row_hbm, current_hbm, out_ref,
    column_ref, inverse_ref, row_ref, current_ref, sems, *, band,
):
    sources = (column_hbm, inverse_hbm, row_hbm, current_hbm)
    targets = (column_ref, inverse_ref, row_ref, current_ref)
    loads = [
        pltpu.make_async_copy(source, target, sems.at[i])
        for i, (source, target) in enumerate(zip(sources, targets))
    ]
    for load in loads:
        load.start()
    rows, cols = current_ref.shape
    order = inverse_ref.shape[0]
    span = rows
    my_rows = place_ref[0] * band
    my_cols = place_ref[1] * (cols // span) * band

    def iota(shape, axis):
        return lax.broadcasted_iota(jnp.int32, shape, axis)

    loads[0].wait()
    shape = (order, rows)
    pick = jnp.where(iota(shape, 0) == iota(shape, 1) + my_rows, -1.0, 0.0)
    column = jnp.where(iota(shape, 1) < band, pick, column_ref[...])
    loads[1].wait()
    scaled = jnp.dot(inverse_ref[...], column, precision=HIGHEST, preferred_element_type=F32).T

    def strip_of(shape):
        at = iota(shape, 1)
        inside = at < band
        within = at
        for g in range(1, cols // span):
            past = at - g * span
            now = (past >= 0) & (past < band)
            inside = inside | now
            within = jnp.where(now, past + g * band, within)
        return inside, within

    shape = (order, cols)
    inside, within = strip_of(shape)
    pick = jnp.where(iota(shape, 0) == within + my_cols, -1.0, 0.0)
    loads[2].wait()
    row = jnp.where(inside, pick, row_ref[...])
    shape = (rows, cols)
    inside, _ = strip_of(shape)
    scaled_high, scaled_low, _ = three_parts(scaled)
    row_high, row_low, _ = three_parts(row)
    change = product(scaled_high, row_high) + (
        product(scaled_high, row_low) + product(scaled_low, row_high)
    )
    loads[3].wait()
    base = jnp.where(inside | (iota(shape, 0) < band), 0.0, current_ref[...])
    out_ref[...] = base - change


def trailing_update(place, current, column, row, inverse, band):
    rows, cols = current.shape
    order = inverse.shape[0]
    return pl.pallas_call(
        functools.partial(update_kernel, band=band),
        out_shape=jax.ShapeDtypeStruct(current.shape, F32),
        in_specs=[pl.BlockSpec(memory_space=pltpu.SMEM)]
        + [pl.BlockSpec(memory_space=pl.ANY)] * 4,
        out_specs=pl.BlockSpec(memory_space=pltpu.VMEM),
        scratch_shapes=[
            pltpu.VMEM(column.shape, F32),
            pltpu.VMEM(inverse.shape, F32),
            pltpu.VMEM(row.shape, F32),
            pltpu.VMEM(current.shape, F32),
            pltpu.SemaphoreType.DMA((4,)),
        ],
        compiler_params=pltpu.CompilerParams(vmem_limit_bytes=56 * 1024 * 1024),
        cost_estimate=pl.CostEstimate(
            flops=2 * rows * order * (cols + order), bytes_accessed=8 * rows * cols, transcendentals=0
        ),
        name="trailing_update",
    )(place, column, inverse, row, current)


def body(matrix):
    rows, cols = matrix.shape
    groups = cols // rows
    depth = lax.axis_size("z")
    chips = lax.axis_size("x") * lax.axis_size("y")
    band = K * B // (2 * chips)
    core = lax.axis_index("c")
    place = jnp.stack([lax.axis_index(("x", "y", "c")), lax.axis_index("z")]).astype(jnp.int32)
    strip = jnp.concatenate(
        [matrix[:, g * rows : g * rows + band] for g in range(groups)], axis=1
    )
    rowband = matrix[0:band, :]
    with jax.named_scope("pivot_z"):
        pivot = lax.all_gather(strip[0:band, :], "z", axis=0, tiled=False)
    own = pivot.transpose(1, 0, 2).reshape(1, band, K * B)
    for axis in ("y", "x"):
        size = lax.axis_size(axis)
        with jax.named_scope("pivot_" + axis):
            pieces = [own] + [
                lax.ppermute(own, axis, [(i, (i + hop) % size) for i in range(size)])
                for hop in range(1, size)
            ]
        own = jnp.concatenate(pieces, axis=0)
    with jax.named_scope("pivot_core"):
        other = lax.ppermute(own, "c", [(0, 1), (1, 0)])
    with jax.named_scope("column_panel"):
        column = lax.all_gather(strip.T, "z", axis=0, tiled=True)
    spread = jnp.broadcast_to(rowband, (2 * chips, band, cols))
    with jax.named_scope("row_panel"):
        row = lax.all_to_all(spread, ("x", "y", "c"), 0, 0)
    hops = jnp.arange(chips, dtype=jnp.int32)
    size_x, size_y = lax.axis_size("x"), lax.axis_size("y")
    from_x = (lax.axis_index("x") - hops // size_y) % size_x
    from_y = (lax.axis_index("y") - hops % size_y) % size_y
    first = 2 * (from_x * size_y + from_y)
    inverse = pivot_inverse(jnp.stack([first + core, first + 1 - core]), own, other)
    return trailing_update(
        place, matrix, column, row.reshape(K * B, cols), inverse, band
    )


def solution(mesh):
    split = Mesh(mesh.devices.reshape(4, 4, 2, 16), ("x", "y", "c", "z"))
    spec = P(("x", "y", "c"), "z")
    return jax.shard_map(body, mesh=split, in_specs=(spec,), out_specs=spec, check_vma=False)
```

```python
import functools

import jax
import jax.numpy as jnp
from jax import lax
from jax.experimental import pallas as pl
from jax.experimental.pallas import tpu as pltpu
from jax.sharding import Mesh
from jax.sharding import PartitionSpec as P

B = 384
K = 2
F32 = jnp.float32
BF16 = jnp.bfloat16
HIGHEST = lax.Precision.HIGHEST
TILE = 128


def lane_splat(tile, lane):
    return jnp.broadcast_to(tile[:, lane : lane + 1], (8, TILE))


def row_splat(tile, row):
    return jnp.broadcast_to(tile[row : row + 1, :], (8, TILE))


def solve_eight(pivot, right):
    size = 8
    pivot = [list(row) for row in pivot]
    right = list(right)
    factor = [[None] * size for _ in range(size)]
    scale = [None] * size
    for j in range(size):
        recip = 1.0 / pivot[j][j]
        scale[j] = recip
        for m in range(j + 1, size):
            factor[m][j] = pivot[m][j] * recip
        for m in range(j + 1, size):
            for q in range(j + 1, m + 1):
                pivot[m][q] = pivot[m][q] - (pivot[m][j] * pivot[q][j]) * recip
            right[m] = right[m] - factor[m][j] * right[j]
    for j in range(size):
        right[j] = right[j] * scale[j]
    for j in reversed(range(size)):
        for m in range(j):
            right[m] = right[m] - factor[j][m] * right[j]
    return right


def invert_tile(rows):
    lane = lax.broadcasted_iota(jnp.int32, (8, TILE), 1)
    sub = lax.broadcasted_iota(jnp.int32, (8, TILE), 0)
    groups = len(rows)
    rows = list(rows)
    for g in range(groups):
        first = 8 * g
        here = rows[g]
        inside = (lane >= first) & (lane < first + 8)
        columns = [lane_splat(here, first + j) for j in range(8)]
        pivot = [[row_splat(columns[j], i) for j in range(i + 1)] for i in range(8)]
        start = jnp.where(inside, jnp.where(lane == first + sub, 1.0, 0.0), here)
        solved = solve_eight(pivot, [row_splat(start, i) for i in range(8)])
        for step in range(1, groups):
            i = (g + step) % groups
            terms = [lane_splat(rows[i], first + j) * solved[j] for j in range(8)]
            while len(terms) > 1:
                terms = [terms[2 * q] + terms[2 * q + 1] for q in range(len(terms) // 2)]
            rows[i] = jnp.where(inside, 0.0, rows[i]) - terms[0]
        merged = solved[0]
        for j in range(1, 8):
            merged = jnp.where(sub == j, solved[j], merged)
        rows[g] = merged
    return rows


def three_parts(value):
    high = value.astype(BF16)
    rest = value - high.astype(F32)
    middle = rest.astype(BF16)
    return high, middle, (rest - middle.astype(F32)).astype(BF16)


def left_parts(value):
    high, middle, low = three_parts(value)
    return jnp.concatenate([high, high, middle, high, low, middle], axis=1)


def right_parts(value):
    high, middle, low = three_parts(value)
    return jnp.concatenate([high, middle, high, low, high, middle], axis=0)


def product(left, right):
    return jnp.dot(left, right, preferred_element_type=F32)


def eliminate(first, last, out_ref, left_ref, right_ref, diagonal_ref):
    order = out_ref.shape[0]
    blocks = order // TILE
    unit = lax.broadcasted_iota(jnp.int32, (TILE, TILE), 0) == lax.broadcasted_iota(
        jnp.int32, (TILE, TILE), 1
    )
    unit = jnp.where(unit, 1.0, 0.0)
    start = slice(TILE * first, TILE * first + TILE)
    diagonal_ref[...] = out_ref[start, start]
    left_ref[...] = jnp.zeros(left_ref.shape, BF16)
    right_ref[...] = jnp.zeros(right_ref.shape, BF16)

    def apply_last():
        for c in range(blocks):
            here = slice(TILE * c, TILE * c + TILE)
            out_ref[:, here] = out_ref[:, here] - product(left_ref[...], right_ref[:, here])

    def step(k, carry):
        here = pl.ds(pl.multiple_of(k * TILE, TILE), TILE)
        apply_last()
        block = diagonal_ref[...]
        rows = invert_tile([block[8 * i : 8 * i + 8, :] for i in range(TILE // 8)])
        inverse = jnp.concatenate(rows, axis=0)
        row = out_ref[here, :]
        out_ref[here, here] = -unit
        column = out_ref[:, here]
        out_ref[:, here] = jnp.zeros((order, TILE), F32)
        left_ref[...] = left_parts(product(left_parts(column), right_parts(inverse)))
        right_ref[...] = right_parts(row)
        right_ref[:, here] = right_parts(unit)
        out_ref[here, :] = jnp.zeros((TILE, order), F32)
        after = pl.ds(pl.multiple_of(jnp.minimum(k + 1, blocks - 1) * TILE, TILE), TILE)
        diagonal_ref[...] = out_ref[after, after] - product(left_ref[after, :], right_ref[:, after])
        return carry

    lax.fori_loop(first, last, step, 0)
    apply_last()


def first_kernel(slot_ref, own_ref, other_ref, out_ref, *scratch, last):
    pairs, band, _ = own_ref.shape
    for i in range(pairs):
        out_ref[pl.ds(pl.multiple_of(slot_ref[0, i] * band, 8), band), :] = own_ref[i]
        out_ref[pl.ds(pl.multiple_of(slot_ref[1, i] * band, 8), band), :] = other_ref[i]
    eliminate(0, last, out_ref, *scratch)


def second_kernel(part_ref, out_ref, *scratch, first):
    out_ref[...] = part_ref[...]
    eliminate(first, out_ref.shape[0] // TILE, out_ref, *scratch)


def pivot_sweep(kernel, order, flops, name, *arrays):
    vmem = pl.BlockSpec(memory_space=pltpu.VMEM)
    small = pl.BlockSpec(memory_space=pltpu.SMEM)
    return pl.pallas_call(
        kernel,
        out_shape=jax.ShapeDtypeStruct((order, order), F32),
        in_specs=[small if array.dtype == jnp.int32 else vmem for array in arrays],
        out_specs=vmem,
        scratch_shapes=[
            pltpu.VMEM((order, 6 * TILE), BF16),
            pltpu.VMEM((6 * TILE, order), BF16),
            pltpu.VMEM((TILE, TILE), F32),
        ],
        compiler_params=pltpu.CompilerParams(vmem_limit_bytes=20 * 1024 * 1024),
        cost_estimate=pl.CostEstimate(flops=flops, bytes_accessed=8, transcendentals=0),
        name=name,
    )(*arrays)


def update_kernel(
    place_ref, column_hbm, inverse_hbm, row_hbm, current_hbm, out_ref,
    column_ref, inverse_ref, row_ref, current_ref, sems, *, band,
):
    sources = (column_hbm, inverse_hbm, row_hbm, current_hbm)
    targets = (column_ref, inverse_ref, row_ref, current_ref)
    loads = [
        pltpu.make_async_copy(source, target, sems.at[i])
        for i, (source, target) in enumerate(zip(sources, targets))
    ]
    for load in loads:
        load.start()
    rows, cols = current_ref.shape
    order = inverse_ref.shape[0]
    span = rows
    my_rows = place_ref[0] * band
    my_cols = place_ref[1] * (cols // span) * band

    def iota(shape, axis):
        return lax.broadcasted_iota(jnp.int32, shape, axis)

    loads[0].wait()
    shape = (order, rows)
    pick = jnp.where(iota(shape, 0) == iota(shape, 1) + my_rows, -1.0, 0.0)
    column = jnp.where(iota(shape, 1) < band, pick, column_ref[...])
    loads[1].wait()
    scaled = jnp.dot(inverse_ref[...], column, precision=HIGHEST, preferred_element_type=F32).T

    def strip_of(shape):
        at = iota(shape, 1)
        inside = at < band
        within = at
        for g in range(1, cols // span):
            past = at - g * span
            now = (past >= 0) & (past < band)
            inside = inside | now
            within = jnp.where(now, past + g * band, within)
        return inside, within

    shape = (order, cols)
    inside, within = strip_of(shape)
    pick = jnp.where(iota(shape, 0) == within + my_cols, -1.0, 0.0)
    loads[2].wait()
    row = jnp.where(inside, pick, row_ref[...])
    shape = (rows, cols)
    inside, _ = strip_of(shape)
    scaled_high, scaled_low, _ = three_parts(scaled)
    row_high, row_low, _ = three_parts(row)
    change = product(scaled_high, row_high) + (
        product(scaled_high, row_low) + product(scaled_low, row_high)
    )
    loads[3].wait()
    base = jnp.where(inside | (iota(shape, 0) < band), 0.0, current_ref[...])
    out_ref[...] = base - change


def trailing_update(place, current, column, row, inverse, band):
    rows, cols = current.shape
    order = inverse.shape[0]
    return pl.pallas_call(
        functools.partial(update_kernel, band=band),
        out_shape=jax.ShapeDtypeStruct(current.shape, F32),
        in_specs=[pl.BlockSpec(memory_space=pltpu.SMEM)]
        + [pl.BlockSpec(memory_space=pl.ANY)] * 4,
        out_specs=pl.BlockSpec(memory_space=pltpu.VMEM),
        scratch_shapes=[
            pltpu.VMEM(column.shape, F32),
            pltpu.VMEM(inverse.shape, F32),
            pltpu.VMEM(row.shape, F32),
            pltpu.VMEM(current.shape, F32),
            pltpu.SemaphoreType.DMA((4,)),
        ],
        compiler_params=pltpu.CompilerParams(vmem_limit_bytes=56 * 1024 * 1024),
        cost_estimate=pl.CostEstimate(
            flops=2 * rows * order * (cols + order), bytes_accessed=8 * rows * cols, transcendentals=0
        ),
        name="trailing_update",
    )(place, column, inverse, row, current)


def body(matrix):
    rows, cols = matrix.shape
    groups = cols // rows
    depth = lax.axis_size("z")
    chips = lax.axis_size("x") * lax.axis_size("y")
    band = K * B // (2 * chips)
    core = lax.axis_index("c")
    place = jnp.stack([lax.axis_index(("x", "y", "c")), lax.axis_index("z")]).astype(jnp.int32)
    strip = jnp.concatenate(
        [matrix[:, g * rows : g * rows + band] for g in range(groups)], axis=1
    )
    rowband = matrix[0:band, :]
    with jax.named_scope("pivot_z"):
        pivot = lax.all_to_all(
            jnp.broadcast_to(strip[0:band, :], (depth, band, groups * band)), "z", 0, 0
        )
    pivot = pivot.transpose(1, 0, 2).reshape(band, K * B)
    with jax.named_scope("pivot_xy"):
        own = lax.all_to_all(jnp.broadcast_to(pivot, (chips, band, K * B)), ("x", "y"), 0, 0)
    with jax.named_scope("pivot_core"):
        other = lax.ppermute(own, "c", [(0, 1), (1, 0)])
    with jax.named_scope("column_panel"):
        column = lax.all_gather(strip.T, "z", axis=0, tiled=True)
    spread = jnp.broadcast_to(rowband, (2 * chips, band, cols))
    spread, other = lax.optimization_barrier((spread, other))
    with jax.named_scope("row_panel"):
        row = lax.all_to_all(spread, ("x", "y", "c"), 0, 0)
    first = 2 * jnp.arange(chips, dtype=jnp.int32)
    slots = jnp.stack([first + core, first + 1 - core])
    order = K * B
    half = 2
    part = pivot_sweep(
        functools.partial(first_kernel, last=half), order, 1, "sweep_first", slots, own, other
    )
    column, part = lax.optimization_barrier((column, part))
    inverse = pivot_sweep(
        functools.partial(second_kernel, first=half), order, 10**12, "sweep_second", part
    )
    return trailing_update(
        place, matrix, column, row.reshape(K * B, cols), inverse, band
    )


def solution(mesh):
    split = Mesh(mesh.devices.reshape(4, 4, 2, 16), ("x", "y", "c", "z"))
    spec = P(("x", "y", "c"), "z")
    return jax.shard_map(body, mesh=split, in_specs=(spec,), out_specs=spec, check_vma=False)
```

```python
import functools

import jax
import jax.numpy as jnp
from jax import lax
from jax.experimental import pallas as pl
from jax.experimental.pallas import tpu as pltpu
from jax.sharding import Mesh
from jax.sharding import PartitionSpec as P

B = 384
K = 2
F32 = jnp.float32
BF16 = jnp.bfloat16
HIGHEST = lax.Precision.HIGHEST
TILE = 128


def lane_splat(tile, lane):
    return jnp.broadcast_to(tile[:, lane : lane + 1], (8, TILE))


def row_splat(tile, row):
    return jnp.broadcast_to(tile[row : row + 1, :], (8, TILE))


def solve_eight(pivot, right):
    size = 8
    pivot = [list(row) for row in pivot]
    right = list(right)
    factor = [[None] * size for _ in range(size)]
    scale = [None] * size
    for j in range(size):
        recip = 1.0 / pivot[j][j]
        scale[j] = recip
        for m in range(j + 1, size):
            factor[m][j] = pivot[m][j] * recip
        for m in range(j + 1, size):
            for q in range(j + 1, m + 1):
                pivot[m][q] = pivot[m][q] - (pivot[m][j] * pivot[q][j]) * recip
            right[m] = right[m] - factor[m][j] * right[j]
    for j in range(size):
        right[j] = right[j] * scale[j]
    for j in reversed(range(size)):
        for m in range(j):
            right[m] = right[m] - factor[j][m] * right[j]
    return right


def invert_tile(rows):
    lane = lax.broadcasted_iota(jnp.int32, (8, TILE), 1)
    sub = lax.broadcasted_iota(jnp.int32, (8, TILE), 0)
    groups = len(rows)
    rows = list(rows)
    for g in range(groups):
        first = 8 * g
        here = rows[g]
        inside = (lane >= first) & (lane < first + 8)
        columns = [lane_splat(here, first + j) for j in range(8)]
        pivot = [[row_splat(columns[j], i) for j in range(i + 1)] for i in range(8)]
        start = jnp.where(inside, jnp.where(lane == first + sub, 1.0, 0.0), here)
        solved = solve_eight(pivot, [row_splat(start, i) for i in range(8)])
        for step in range(1, groups):
            i = (g + step) % groups
            terms = [lane_splat(rows[i], first + j) * solved[j] for j in range(8)]
            while len(terms) > 1:
                terms = [terms[2 * q] + terms[2 * q + 1] for q in range(len(terms) // 2)]
            rows[i] = jnp.where(inside, 0.0, rows[i]) - terms[0]
        merged = solved[0]
        for j in range(1, 8):
            merged = jnp.where(sub == j, solved[j], merged)
        rows[g] = merged
    return rows


def three_parts(value):
    high = value.astype(BF16)
    rest = value - high.astype(F32)
    middle = rest.astype(BF16)
    return high, middle, (rest - middle.astype(F32)).astype(BF16)


def left_parts(value):
    high, middle, low = three_parts(value)
    return jnp.concatenate([high, high, middle, high, low, middle], axis=1)


def right_parts(value):
    high, middle, low = three_parts(value)
    return jnp.concatenate([high, middle, high, low, high, middle], axis=0)


def product(left, right):
    return jnp.dot(left, right, preferred_element_type=F32)


def eliminate(first, last, done, out_ref, left_ref, right_ref, diagonal_ref):
    order = out_ref.shape[0]
    blocks = order // TILE
    unit = lax.broadcasted_iota(jnp.int32, (TILE, TILE), 0) == lax.broadcasted_iota(
        jnp.int32, (TILE, TILE), 1
    )
    unit = jnp.where(unit, 1.0, 0.0)
    start = slice(TILE * first, TILE * first + TILE)
    diagonal_ref[...] = out_ref[start, start]
    left_ref[...] = jnp.zeros(left_ref.shape, BF16)
    right_ref[...] = jnp.zeros(right_ref.shape, BF16)

    def apply_last(done=None):
        for c in range(blocks):
            here = slice(TILE * c, TILE * c + TILE)
            out_ref[:, here] = out_ref[:, here] - product(left_ref[...], right_ref[:, here])
            if done is not None:
                done(here)

    def step(k, carry):
        here = pl.ds(pl.multiple_of(k * TILE, TILE), TILE)
        apply_last()
        block = diagonal_ref[...]
        rows = invert_tile([block[8 * i : 8 * i + 8, :] for i in range(TILE // 8)])
        inverse = jnp.concatenate(rows, axis=0)
        row = out_ref[here, :]
        out_ref[here, here] = -unit
        column = out_ref[:, here]
        out_ref[:, here] = jnp.zeros((order, TILE), F32)
        left_ref[...] = left_parts(product(left_parts(column), right_parts(inverse)))
        right_ref[...] = right_parts(row)
        right_ref[:, here] = right_parts(unit)
        out_ref[here, :] = jnp.zeros((TILE, order), F32)
        after = pl.ds(pl.multiple_of(jnp.minimum(k + 1, blocks - 1) * TILE, TILE), TILE)
        diagonal_ref[...] = out_ref[after, after] - product(left_ref[after, :], right_ref[:, after])
        return carry

    lax.fori_loop(first, last, step, 0)
    apply_last(done)


def sweep_kernel(*refs, first, last, joined):
    out_hbm, left_ref, right_ref, diagonal_ref, work_ref, sem = refs[-6:]
    if joined:
        work_ref[...] = refs[0][...]
    else:
        slot_ref, own_ref, other_ref = refs[:3]
        pairs, band, _ = own_ref.shape
        for i in range(pairs):
            work_ref[pl.ds(pl.multiple_of(slot_ref[0, i] * band, 8), band), :] = own_ref[i]
            work_ref[pl.ds(pl.multiple_of(slot_ref[1, i] * band, 8), band), :] = other_ref[i]

    def store(here):
        pltpu.make_async_copy(work_ref.at[:, here], out_hbm.at[:, here], sem).start()

    eliminate(first, last, store, work_ref, left_ref, right_ref, diagonal_ref)
    pltpu.make_async_copy(work_ref, out_hbm, sem).wait()


def pivot_sweep(first, last, order, flops, name, *arrays):
    vmem = pl.BlockSpec(memory_space=pltpu.VMEM)
    small = pl.BlockSpec(memory_space=pltpu.SMEM)
    return pl.pallas_call(
        functools.partial(sweep_kernel, first=first, last=last, joined=len(arrays) == 1),
        out_shape=jax.ShapeDtypeStruct((order, order), F32),
        in_specs=[small if array.dtype == jnp.int32 else vmem for array in arrays],
        out_specs=pl.BlockSpec(memory_space=pl.ANY),
        scratch_shapes=[
            pltpu.VMEM((order, 6 * TILE), BF16),
            pltpu.VMEM((6 * TILE, order), BF16),
            pltpu.VMEM((TILE, TILE), F32),
            pltpu.VMEM((order, order), F32),
            pltpu.SemaphoreType.DMA(()),
        ],
        compiler_params=pltpu.CompilerParams(vmem_limit_bytes=54 * 1024 * 1024),
        cost_estimate=pl.CostEstimate(flops=flops, bytes_accessed=8, transcendentals=0),
        name=name,
    )(*arrays)


def update_kernel(
    place_ref, column_hbm, inverse_hbm, row_hbm, current_hbm, out_ref,
    column_ref, inverse_ref, row_ref, current_ref, sems, *, band,
):
    sources = (column_hbm, inverse_hbm, row_hbm, current_hbm)
    targets = (column_ref, inverse_ref, row_ref, current_ref)
    loads = [
        pltpu.make_async_copy(source, target, sems.at[i])
        for i, (source, target) in enumerate(zip(sources, targets))
    ]
    for load in loads:
        load.start()
    rows, cols = current_ref.shape
    order = inverse_ref.shape[0]
    span = rows
    my_rows = place_ref[0] * band
    my_cols = place_ref[1] * (cols // span) * band

    def iota(shape, axis):
        return lax.broadcasted_iota(jnp.int32, shape, axis)

    loads[0].wait()
    shape = (order, rows)
    pick = jnp.where(iota(shape, 0) == iota(shape, 1) + my_rows, -1.0, 0.0)
    column = jnp.where(iota(shape, 1) < band, pick, column_ref[...])
    loads[1].wait()
    scaled = product(left_parts(inverse_ref[...]), right_parts(column)).T

    def strip_of(shape):
        at = iota(shape, 1)
        inside = at < band
        within = at
        for g in range(1, cols // span):
            past = at - g * span
            now = (past >= 0) & (past < band)
            inside = inside | now
            within = jnp.where(now, past + g * band, within)
        return inside, within

    shape = (order, cols)
    inside, within = strip_of(shape)
    pick = jnp.where(iota(shape, 0) == within + my_cols, -1.0, 0.0)
    loads[2].wait()
    row = jnp.where(inside, pick, row_ref[...])
    shape = (rows, cols)
    inside, _ = strip_of(shape)
    scaled_high, scaled_low, _ = three_parts(scaled)
    row_high, row_low, _ = three_parts(row)
    change = product(
        jnp.concatenate([scaled_high, scaled_high, scaled_low], axis=1),
        jnp.concatenate([row_high, row_low, row_high], axis=0),
    )
    loads[3].wait()
    base = jnp.where(inside | (iota(shape, 0) < band), 0.0, current_ref[...])
    out_ref[...] = base - change


def trailing_update(place, current, column, row, inverse, band):
    rows, cols = current.shape
    order = inverse.shape[0]
    return pl.pallas_call(
        functools.partial(update_kernel, band=band),
        out_shape=jax.ShapeDtypeStruct(current.shape, F32),
        in_specs=[pl.BlockSpec(memory_space=pltpu.SMEM)]
        + [pl.BlockSpec(memory_space=pl.ANY)] * 4,
        out_specs=pl.BlockSpec(memory_space=pltpu.VMEM),
        scratch_shapes=[
            pltpu.VMEM(column.shape, F32),
            pltpu.VMEM(inverse.shape, F32),
            pltpu.VMEM(row.shape, F32),
            pltpu.VMEM(current.shape, F32),
            pltpu.SemaphoreType.DMA((4,)),
        ],
        compiler_params=pltpu.CompilerParams(vmem_limit_bytes=56 * 1024 * 1024),
        cost_estimate=pl.CostEstimate(
            flops=2 * rows * order * (cols + order), bytes_accessed=8 * rows * cols, transcendentals=0
        ),
        name="trailing_update",
    )(place, column, inverse, row, current)


def body(matrix):
    rows, cols = matrix.shape
    groups = cols // rows
    depth = lax.axis_size("z")
    chips = lax.axis_size("x") * lax.axis_size("y")
    band = K * B // (2 * chips)
    core = lax.axis_index("c")
    place = jnp.stack([lax.axis_index(("x", "y", "c")), lax.axis_index("z")]).astype(jnp.int32)
    strip = jnp.concatenate(
        [matrix[:, g * rows : g * rows + band] for g in range(groups)], axis=1
    )
    rowband = matrix[0:band, :]
    with jax.named_scope("pivot_z"):
        padded = jnp.pad(strip[0:band, :], ((0, 0), (0, TILE - groups * band)))
        pivot = lax.all_to_all(jnp.broadcast_to(padded, (depth, band, TILE)), "z", 0, 0)
    pivot = pivot[:, :, : groups * band].transpose(1, 0, 2).reshape(band, K * B)
    with jax.named_scope("pivot_xy"):
        own = lax.all_to_all(jnp.broadcast_to(pivot, (chips, band, K * B)), ("x", "y"), 0, 0)
    with jax.named_scope("pivot_core"):
        other = lax.ppermute(own, "c", [(0, 1), (1, 0)])
    with jax.named_scope("column_panel"):
        column = lax.all_gather(strip.T, "z", axis=0, tiled=True)
    spread = jnp.broadcast_to(rowband, (2 * chips, band, cols))
    spread, other = lax.optimization_barrier((spread, other))
    with jax.named_scope("row_panel"):
        row = lax.all_to_all(spread, ("x", "y", "c"), 0, 0)
    first = 2 * jnp.arange(chips, dtype=jnp.int32)
    slots = jnp.stack([first + core, first + 1 - core])
    order = K * B
    half = 4
    blocks = order // TILE
    part = pivot_sweep(0, half, order, 1, "sweep_first", slots, own, other)
    column, part = lax.optimization_barrier((column, part))
    inverse = pivot_sweep(half, blocks, order, 24 * 10**9, "sweep_second", part)
    return trailing_update(
        place, matrix, column, row.reshape(K * B, cols), inverse, band
    )


def solution(mesh):
    split = Mesh(mesh.devices.reshape(4, 4, 2, 16), ("x", "y", "c", "z"))
    spec = P(("x", "y", "c"), "z")
    return jax.shard_map(body, mesh=split, in_specs=(spec,), out_specs=spec, check_vma=False)
```

```python
import functools

import jax
import jax.numpy as jnp
from jax import lax
from jax.experimental import pallas as pl
from jax.experimental.pallas import tpu as pltpu
from jax.sharding import Mesh
from jax.sharding import PartitionSpec as P

B = 384
K = 2
F32 = jnp.float32
BF16 = jnp.bfloat16
HIGHEST = lax.Precision.HIGHEST
TILE = 128


def lane_splat(tile, lane):
    return jnp.broadcast_to(tile[:, lane : lane + 1], (8, TILE))


def row_splat(tile, row):
    return jnp.broadcast_to(tile[row : row + 1, :], (8, TILE))


def solve_eight(pivot, right):
    size = 8
    pivot = [list(row) for row in pivot]
    right = list(right)
    factor = [[None] * size for _ in range(size)]
    scale = [None] * size
    for j in range(size):
        recip = 1.0 / pivot[j][j]
        scale[j] = recip
        for m in range(j + 1, size):
            factor[m][j] = pivot[m][j] * recip
        for m in range(j + 1, size):
            for q in range(j + 1, m + 1):
                pivot[m][q] = pivot[m][q] - (pivot[m][j] * pivot[q][j]) * recip
            right[m] = right[m] - factor[m][j] * right[j]
    for j in range(size):
        right[j] = right[j] * scale[j]
    for j in reversed(range(size)):
        for m in range(j):
            right[m] = right[m] - factor[j][m] * right[j]
    return right


def invert_tile(rows):
    lane = lax.broadcasted_iota(jnp.int32, (8, TILE), 1)
    sub = lax.broadcasted_iota(jnp.int32, (8, TILE), 0)
    groups = len(rows)
    rows = list(rows)
    for g in range(groups):
        first = 8 * g
        here = rows[g]
        inside = (lane >= first) & (lane < first + 8)
        columns = [lane_splat(here, first + j) for j in range(8)]
        pivot = [[row_splat(columns[j], i) for j in range(i + 1)] for i in range(8)]
        start = jnp.where(inside, jnp.where(lane == first + sub, 1.0, 0.0), here)
        solved = solve_eight(pivot, [row_splat(start, i) for i in range(8)])
        for step in range(1, groups):
            i = (g + step) % groups
            terms = [lane_splat(rows[i], first + j) * solved[j] for j in range(8)]
            while len(terms) > 1:
                terms = [terms[2 * q] + terms[2 * q + 1] for q in range(len(terms) // 2)]
            rows[i] = jnp.where(inside, 0.0, rows[i]) - terms[0]
        merged = solved[0]
        for j in range(1, 8):
            merged = jnp.where(sub == j, solved[j], merged)
        rows[g] = merged
    return rows


def three_parts(value):
    high = value.astype(BF16)
    rest = value - high.astype(F32)
    middle = rest.astype(BF16)
    return high, middle, (rest - middle.astype(F32)).astype(BF16)


def left_parts(value):
    high, middle, low = three_parts(value)
    return jnp.concatenate([high, high, middle, high, low, middle], axis=1)


def right_parts(value):
    high, middle, low = three_parts(value)
    return jnp.concatenate([high, middle, high, low, high, middle], axis=0)


def product(left, right):
    return jnp.dot(left, right, preferred_element_type=F32)


def eliminate(first, last, out_ref, left_ref, right_ref, diagonal_ref):
    order = out_ref.shape[0]
    blocks = order // TILE
    unit = lax.broadcasted_iota(jnp.int32, (TILE, TILE), 0) == lax.broadcasted_iota(
        jnp.int32, (TILE, TILE), 1
    )
    unit = jnp.where(unit, 1.0, 0.0)
    start = slice(TILE * first, TILE * first + TILE)
    diagonal_ref[...] = out_ref[start, start]
    left_ref[...] = jnp.zeros(left_ref.shape, BF16)
    right_ref[...] = jnp.zeros(right_ref.shape, BF16)

    def apply_last():
        for c in range(blocks):
            here = slice(TILE * c, TILE * c + TILE)
            out_ref[:, here] = out_ref[:, here] - product(left_ref[...], right_ref[:, here])

    def step(k, carry):
        here = pl.ds(pl.multiple_of(k * TILE, TILE), TILE)
        apply_last()
        block = diagonal_ref[...]
        rows = invert_tile([block[8 * i : 8 * i + 8, :] for i in range(TILE // 8)])
        inverse = jnp.concatenate(rows, axis=0)
        row = out_ref[here, :]
        out_ref[here, here] = -unit
        column = out_ref[:, here]
        out_ref[:, here] = jnp.zeros((order, TILE), F32)
        left_ref[...] = left_parts(product(left_parts(column), right_parts(inverse)))
        right_ref[...] = right_parts(row)
        right_ref[:, here] = right_parts(unit)
        out_ref[here, :] = jnp.zeros((TILE, order), F32)
        after = pl.ds(pl.multiple_of(jnp.minimum(k + 1, blocks - 1) * TILE, TILE), TILE)
        diagonal_ref[...] = out_ref[after, after] - product(left_ref[after, :], right_ref[:, after])
        return carry

    lax.fori_loop(first, last, step, 0)
    apply_last()


def inverse_kernel(slot_ref, own_ref, other_ref, out_ref, left_ref, right_ref, diagonal_ref):
    pairs, band, order = own_ref.shape
    for i in range(pairs):
        out_ref[pl.ds(pl.multiple_of(slot_ref[0, i] * band, 8), band), :] = own_ref[i]
        out_ref[pl.ds(pl.multiple_of(slot_ref[1, i] * band, 8), band), :] = other_ref[i]
    eliminate(0, order // TILE, out_ref, left_ref, right_ref, diagonal_ref)


def pivot_inverse(slots, own, other):
    order = own.shape[2]
    vmem = pl.BlockSpec(memory_space=pltpu.VMEM)
    return pl.pallas_call(
        inverse_kernel,
        out_shape=jax.ShapeDtypeStruct((order, order), F32),
        in_specs=[pl.BlockSpec(memory_space=pltpu.SMEM), vmem, vmem],
        out_specs=vmem,
        scratch_shapes=[
            pltpu.VMEM((order, 6 * TILE), BF16),
            pltpu.VMEM((6 * TILE, order), BF16),
            pltpu.VMEM((TILE, TILE), F32),
        ],
        compiler_params=pltpu.CompilerParams(vmem_limit_bytes=20 * 1024 * 1024),
        cost_estimate=pl.CostEstimate(flops=1, bytes_accessed=8, transcendentals=0),
        name="pivot_inverse",
    )(slots, own, other)


def iota(shape, axis):
    return lax.broadcasted_iota(jnp.int32, shape, axis)


def start_loads(sources, targets, sems):
    loads = [
        pltpu.make_async_copy(source, target, sems.at[i])
        for i, (source, target) in enumerate(zip(sources, targets))
    ]
    for load in loads:
        load.start()
    return loads


def scale_kernel(place_ref, inverse_hbm, column_hbm, out_ref, inverse_ref, column_ref, sems, *, band):
    loads = start_loads((inverse_hbm, column_hbm), (inverse_ref, column_ref), sems)
    shape = column_ref.shape
    loads[0].wait()
    left = left_parts(inverse_ref[...])
    pick = jnp.where(iota(shape, 0) == iota(shape, 1) + place_ref[0] * band, -1.0, 0.0)
    loads[1].wait()
    column = jnp.where(iota(shape, 1) < band, pick, column_ref[...])
    out_ref[...] = product(left, right_parts(column)).T


def update_kernel(
    place_ref, row_hbm, scaled_hbm, current_hbm, out_ref,
    row_ref, scaled_ref, current_ref, sems, *, band,
):
    loads = start_loads(
        (row_hbm, scaled_hbm, current_hbm), (row_ref, scaled_ref, current_ref), sems
    )
    rows, cols = current_ref.shape
    order = row_ref.shape[0]
    span = rows
    my_cols = place_ref[1] * (cols // span) * band

    def strip_of(shape):
        at = iota(shape, 1)
        inside = at < band
        within = at
        for g in range(1, cols // span):
            past = at - g * span
            now = (past >= 0) & (past < band)
            inside = inside | now
            within = jnp.where(now, past + g * band, within)
        return inside, within

    shape = (order, cols)
    inside, within = strip_of(shape)
    pick = jnp.where(iota(shape, 0) == within + my_cols, -1.0, 0.0)
    loads[0].wait()
    row_high, row_low, _ = three_parts(jnp.where(inside, pick, row_ref[...]))
    loads[1].wait()
    scaled_high, scaled_low, _ = three_parts(scaled_ref[...])
    change = product(
        jnp.concatenate([scaled_high, scaled_high, scaled_low], axis=1),
        jnp.concatenate([row_high, row_low, row_high], axis=0),
    )
    shape = (rows, cols)
    inside, _ = strip_of(shape)
    loads[2].wait()
    base = jnp.where(inside | (iota(shape, 0) < band), 0.0, current_ref[...])
    out_ref[...] = base - change


def loading_call(kernel, out_shape, flops, name, place, band, *arrays):
    return pl.pallas_call(
        functools.partial(kernel, band=band),
        out_shape=jax.ShapeDtypeStruct(out_shape, F32),
        in_specs=[pl.BlockSpec(memory_space=pltpu.SMEM)]
        + [pl.BlockSpec(memory_space=pl.ANY)] * len(arrays),
        out_specs=pl.BlockSpec(memory_space=pltpu.VMEM),
        scratch_shapes=[pltpu.VMEM(array.shape, F32) for array in arrays]
        + [pltpu.SemaphoreType.DMA((len(arrays),))],
        compiler_params=pltpu.CompilerParams(vmem_limit_bytes=56 * 1024 * 1024),
        cost_estimate=pl.CostEstimate(flops=flops, bytes_accessed=8, transcendentals=0),
        name=name,
    )(place, *arrays)


def body(matrix):
    rows, cols = matrix.shape
    groups = cols // rows
    depth = lax.axis_size("z")
    chips = lax.axis_size("x") * lax.axis_size("y")
    band = K * B // (2 * chips)
    core = lax.axis_index("c")
    place = jnp.stack([lax.axis_index(("x", "y", "c")), lax.axis_index("z")]).astype(jnp.int32)
    strip = jnp.concatenate(
        [matrix[:, g * rows : g * rows + band] for g in range(groups)], axis=1
    )
    rowband = matrix[0:band, :]
    with jax.named_scope("pivot_z"):
        padded = jnp.pad(strip[0:band, :], ((0, 0), (0, TILE - groups * band)))
        pivot = lax.all_to_all(jnp.broadcast_to(padded, (depth, band, TILE)), "z", 0, 0)
    pivot = pivot[:, :, : groups * band].transpose(1, 0, 2).reshape(band, K * B)
    with jax.named_scope("pivot_xy"):
        own = lax.all_to_all(jnp.broadcast_to(pivot, (chips, band, K * B)), ("x", "y"), 0, 0)
    with jax.named_scope("pivot_core"):
        other = lax.ppermute(own, "c", [(0, 1), (1, 0)])
    with jax.named_scope("column_panel"):
        column = lax.all_gather(strip.T, "z", axis=0, tiled=True)
    spread = jnp.broadcast_to(rowband, (2 * chips, band, cols))
    spread, other = lax.optimization_barrier((spread, other))
    with jax.named_scope("row_panel"):
        row = lax.all_to_all(spread, ("x", "y", "c"), 0, 0)
    first = 2 * jnp.arange(chips, dtype=jnp.int32)
    slots = jnp.stack([first + core, first + 1 - core])
    order = K * B
    inverse = pivot_inverse(slots, own, other)
    scaled = loading_call(
        scale_kernel, (rows, order), 24*10**9, "scale", place, band, inverse, column
    )
    row = row.reshape(order, cols)
    return loading_call(
        update_kernel, (rows, cols), 1, "trailing_update", place, band, row, scaled, matrix
    )


def solution(mesh):
    split = Mesh(mesh.devices.reshape(4, 4, 2, 16), ("x", "y", "c", "z"))
    spec = P(("x", "y", "c"), "z")
    return jax.shard_map(body, mesh=split, in_specs=(spec,), out_specs=spec, check_vma=False)
```

```python
import functools

import jax
import jax.numpy as jnp
from jax import lax
from jax.experimental import pallas as pl
from jax.experimental.pallas import tpu as pltpu
from jax.sharding import Mesh
from jax.sharding import PartitionSpec as P

B = 384
K = 2
F32 = jnp.float32
BF16 = jnp.bfloat16
HIGHEST = lax.Precision.HIGHEST
TILE = 128


def lane_splat(tile, lane):
    return jnp.broadcast_to(tile[:, lane : lane + 1], (8, TILE))


def row_splat(tile, row):
    return jnp.broadcast_to(tile[row : row + 1, :], (8, TILE))


def solve_eight(pivot, right):
    size = 8
    pivot = [list(row) for row in pivot]
    right = list(right)
    factor = [[None] * size for _ in range(size)]
    scale = [None] * size
    for j in range(size):
        recip = 1.0 / pivot[j][j]
        scale[j] = recip
        for m in range(j + 1, size):
            factor[m][j] = pivot[m][j] * recip
        for m in range(j + 1, size):
            for q in range(j + 1, m + 1):
                pivot[m][q] = pivot[m][q] - (pivot[m][j] * pivot[q][j]) * recip
            right[m] = right[m] - factor[m][j] * right[j]
    for j in range(size):
        right[j] = right[j] * scale[j]
    for j in reversed(range(size)):
        for m in range(j):
            right[m] = right[m] - factor[j][m] * right[j]
    return right


def invert_tile(rows):
    lane = lax.broadcasted_iota(jnp.int32, (8, TILE), 1)
    sub = lax.broadcasted_iota(jnp.int32, (8, TILE), 0)
    groups = len(rows)
    rows = list(rows)
    for g in range(groups):
        first = 8 * g
        here = rows[g]
        inside = (lane >= first) & (lane < first + 8)
        columns = [lane_splat(here, first + j) for j in range(8)]
        pivot = [[row_splat(columns[j], i) for j in range(i + 1)] for i in range(8)]
        start = jnp.where(inside, jnp.where(lane == first + sub, 1.0, 0.0), here)
        solved = solve_eight(pivot, [row_splat(start, i) for i in range(8)])
        for step in range(1, groups):
            i = (g + step) % groups
            terms = [lane_splat(rows[i], first + j) * solved[j] for j in range(8)]
            while len(terms) > 1:
                terms = [terms[2 * q] + terms[2 * q + 1] for q in range(len(terms) // 2)]
            rows[i] = jnp.where(inside, 0.0, rows[i]) - terms[0]
        merged = solved[0]
        for j in range(1, 8):
            merged = jnp.where(sub == j, solved[j], merged)
        rows[g] = merged
    return rows


def three_parts(value):
    high = value.astype(BF16)
    rest = value - high.astype(F32)
    middle = rest.astype(BF16)
    return high, middle, (rest - middle.astype(F32)).astype(BF16)


def left_parts(value):
    high, middle, low = three_parts(value)
    return jnp.concatenate([high, high, middle, high, low, middle], axis=1)


def right_parts(value):
    high, middle, low = three_parts(value)
    return jnp.concatenate([high, middle, high, low, high, middle], axis=0)


def product(left, right):
    return jnp.dot(left, right, preferred_element_type=F32)


def eliminate(first, last, out_ref, left_ref, right_ref, diagonal_ref):
    order = out_ref.shape[0]
    blocks = order // TILE
    unit = lax.broadcasted_iota(jnp.int32, (TILE, TILE), 0) == lax.broadcasted_iota(
        jnp.int32, (TILE, TILE), 1
    )
    unit = jnp.where(unit, 1.0, 0.0)
    start = slice(TILE * first, TILE * first + TILE)
    diagonal_ref[...] = out_ref[start, start]
    left_ref[...] = jnp.zeros(left_ref.shape, BF16)
    right_ref[...] = jnp.zeros(right_ref.shape, BF16)

    def apply_last():
        for c in range(blocks):
            here = slice(TILE * c, TILE * c + TILE)
            out_ref[:, here] = out_ref[:, here] - product(left_ref[...], right_ref[:, here])

    def step(k, carry):
        here = pl.ds(pl.multiple_of(k * TILE, TILE), TILE)
        apply_last()
        block = diagonal_ref[...]
        rows = invert_tile([block[8 * i : 8 * i + 8, :] for i in range(TILE // 8)])
        inverse = jnp.concatenate(rows, axis=0)
        row = out_ref[here, :]
        out_ref[here, here] = -unit
        column = out_ref[:, here]
        out_ref[:, here] = jnp.zeros((order, TILE), F32)
        left_ref[...] = left_parts(product(left_parts(column), right_parts(inverse)))
        right_ref[...] = right_parts(row)
        right_ref[:, here] = right_parts(unit)
        out_ref[here, :] = jnp.zeros((TILE, order), F32)
        after = pl.ds(pl.multiple_of(jnp.minimum(k + 1, blocks - 1) * TILE, TILE), TILE)
        diagonal_ref[...] = out_ref[after, after] - product(left_ref[after, :], right_ref[:, after])
        return carry

    lax.fori_loop(first, last, step, 0)
    apply_last()


def inverse_kernel(slot_ref, own_ref, other_ref, out_ref, left_ref, right_ref, diagonal_ref):
    pairs, band, order = own_ref.shape
    for i in range(pairs):
        out_ref[pl.ds(pl.multiple_of(slot_ref[0, i] * band, 8), band), :] = own_ref[i]
        out_ref[pl.ds(pl.multiple_of(slot_ref[1, i] * band, 8), band), :] = other_ref[i]
    eliminate(0, order // TILE, out_ref, left_ref, right_ref, diagonal_ref)


def pivot_inverse(slots, own, other):
    order = own.shape[2]
    vmem = pl.BlockSpec(memory_space=pltpu.VMEM)
    return pl.pallas_call(
        inverse_kernel,
        out_shape=jax.ShapeDtypeStruct((order, order), F32),
        in_specs=[pl.BlockSpec(memory_space=pltpu.SMEM), vmem, vmem],
        out_specs=vmem,
        scratch_shapes=[
            pltpu.VMEM((order, 6 * TILE), BF16),
            pltpu.VMEM((6 * TILE, order), BF16),
            pltpu.VMEM((TILE, TILE), F32),
        ],
        compiler_params=pltpu.CompilerParams(vmem_limit_bytes=20 * 1024 * 1024),
        cost_estimate=pl.CostEstimate(flops=1, bytes_accessed=8, transcendentals=0),
        name="pivot_inverse",
    )(slots, own, other)


def iota(shape, axis):
    return lax.broadcasted_iota(jnp.int32, shape, axis)


def start_loads(sources, targets, sems):
    loads = [
        pltpu.make_async_copy(source, target, sems.at[i])
        for i, (source, target) in enumerate(zip(sources, targets))
    ]
    for load in loads:
        load.start()
    return loads


def scale_kernel(place_ref, inverse_hbm, column_hbm, out_ref, inverse_ref, column_ref, sems, *, band):
    loads = start_loads((inverse_hbm, column_hbm), (inverse_ref, column_ref), sems)
    shape = column_ref.shape
    loads[0].wait()
    right = right_parts(inverse_ref[...])
    pick = jnp.where(iota(shape, 0) == iota(shape, 1) + place_ref[0] * band, -1.0, 0.0)
    loads[1].wait()
    column = jnp.where(iota(shape, 1) < band, pick, column_ref[...])
    out_ref[...] = product(left_parts(column.T), right)


def update_kernel(
    place_ref, row_hbm, scaled_hbm, current_hbm, out_ref,
    row_ref, scaled_ref, current_ref, sems, *, band,
):
    loads = start_loads(
        (row_hbm, scaled_hbm, current_hbm), (row_ref, scaled_ref, current_ref), sems
    )
    rows, cols = current_ref.shape
    order = row_ref.shape[0]
    span = rows
    my_cols = place_ref[1] * (cols // span) * band

    def strip_of(shape):
        at = iota(shape, 1)
        inside = at < band
        within = at
        for g in range(1, cols // span):
            past = at - g * span
            now = (past >= 0) & (past < band)
            inside = inside | now
            within = jnp.where(now, past + g * band, within)
        return inside, within

    shape = (order, cols)
    inside, within = strip_of(shape)
    pick = jnp.where(iota(shape, 0) == within + my_cols, -1.0, 0.0)
    loads[0].wait()
    row_high, row_low, _ = three_parts(jnp.where(inside, pick, row_ref[...]))
    loads[1].wait()
    scaled_high, scaled_low, _ = three_parts(scaled_ref[...])
    change = product(
        jnp.concatenate([scaled_high, scaled_high, scaled_low], axis=1),
        jnp.concatenate([row_high, row_low, row_high], axis=0),
    )
    shape = (rows, cols)
    inside, _ = strip_of(shape)
    loads[2].wait()
    base = jnp.where(inside | (iota(shape, 0) < band), 0.0, current_ref[...])
    out_ref[...] = base - change


def loading_call(kernel, out_shape, flops, name, place, band, *arrays):
    return pl.pallas_call(
        functools.partial(kernel, band=band),
        out_shape=jax.ShapeDtypeStruct(out_shape, F32),
        in_specs=[pl.BlockSpec(memory_space=pltpu.SMEM)]
        + [pl.BlockSpec(memory_space=pl.ANY)] * len(arrays),
        out_specs=pl.BlockSpec(memory_space=pltpu.VMEM),
        scratch_shapes=[pltpu.VMEM(array.shape, F32) for array in arrays]
        + [pltpu.SemaphoreType.DMA((len(arrays),))],
        compiler_params=pltpu.CompilerParams(vmem_limit_bytes=56 * 1024 * 1024),
        cost_estimate=pl.CostEstimate(flops=flops, bytes_accessed=8, transcendentals=0),
        name=name,
    )(place, *arrays)


def body(matrix):
    rows, cols = matrix.shape
    groups = cols // rows
    depth = lax.axis_size("z")
    chips = lax.axis_size("x") * lax.axis_size("y")
    band = K * B // (2 * chips)
    core = lax.axis_index("c")
    place = jnp.stack([lax.axis_index(("x", "y", "c")), lax.axis_index("z")]).astype(jnp.int32)
    strip = jnp.concatenate(
        [matrix[:, g * rows : g * rows + band] for g in range(groups)], axis=1
    )
    rowband = matrix[0:band, :]
    with jax.named_scope("pivot_z"):
        padded = jnp.pad(strip[0:band, :], ((0, 0), (0, TILE - groups * band)))
        pivot = lax.all_to_all(jnp.broadcast_to(padded, (depth, band, TILE)), "z", 0, 0)
    pivot = pivot[:, :, : groups * band].transpose(1, 0, 2).reshape(band, K * B)
    with jax.named_scope("pivot_xy"):
        own = lax.all_to_all(jnp.broadcast_to(pivot, (chips, band, K * B)), ("x", "y"), 0, 0)
    with jax.named_scope("column_panel"):
        column = lax.all_gather(strip.T, "z", axis=0, tiled=True)
    spread = jnp.broadcast_to(rowband, (2 * chips, band, cols))
    spread, own = lax.optimization_barrier((spread, own))
    with jax.named_scope("pivot_core"):
        other = lax.ppermute(own, "c", [(0, 1), (1, 0)])
    with jax.named_scope("row_panel"):
        row = lax.all_to_all(spread, ("x", "y", "c"), 0, 0)
    first = 2 * jnp.arange(chips, dtype=jnp.int32)
    slots = jnp.stack([first + core, first + 1 - core])
    order = K * B
    inverse = pivot_inverse(slots, own, other)
    scaled = loading_call(
        scale_kernel, (rows, order), 24*10**9, "scale", place, band, inverse, column
    )
    row = row.reshape(order, cols)
    return loading_call(
        update_kernel, (rows, cols), 1, "trailing_update", place, band, row, scaled, matrix
    )


def solution(mesh):
    split = Mesh(mesh.devices.reshape(4, 4, 2, 16), ("x", "y", "c", "z"))
    spec = P(("x", "y", "c"), "z")
    return jax.shard_map(body, mesh=split, in_specs=(spec,), out_specs=spec, check_vma=False)
```

```python
import functools

import jax
import jax.numpy as jnp
from jax import lax
from jax.experimental import pallas as pl
from jax.experimental.pallas import tpu as pltpu
from jax.sharding import Mesh
from jax.sharding import PartitionSpec as P

B = 384
K = 2
F32 = jnp.float32
BF16 = jnp.bfloat16
HIGHEST = lax.Precision.HIGHEST
TILE = 128


def lane_splat(tile, lane):
    return jnp.broadcast_to(tile[:, lane : lane + 1], (8, TILE))


def row_splat(tile, row):
    return jnp.broadcast_to(tile[row : row + 1, :], (8, TILE))


def solve_eight(pivot, right):
    size = 8
    pivot = [list(row) for row in pivot]
    right = list(right)
    factor = [[None] * size for _ in range(size)]
    scale = [None] * size
    for j in range(size):
        recip = 1.0 / pivot[j][j]
        scale[j] = recip
        for m in range(j + 1, size):
            factor[m][j] = pivot[m][j] * recip
        for m in range(j + 1, size):
            for q in range(j + 1, m + 1):
                pivot[m][q] = pivot[m][q] - (pivot[m][j] * pivot[q][j]) * recip
            right[m] = right[m] - factor[m][j] * right[j]
    for j in range(size):
        right[j] = right[j] * scale[j]
    for j in reversed(range(size)):
        for m in range(j):
            right[m] = right[m] - factor[j][m] * right[j]
    return right


def invert_tile(rows):
    lane = lax.broadcasted_iota(jnp.int32, (8, TILE), 1)
    sub = lax.broadcasted_iota(jnp.int32, (8, TILE), 0)
    groups = len(rows)
    rows = list(rows)
    for g in range(groups):
        first = 8 * g
        here = rows[g]
        inside = (lane >= first) & (lane < first + 8)
        columns = [lane_splat(here, first + j) for j in range(8)]
        pivot = [[row_splat(columns[j], i) for j in range(i + 1)] for i in range(8)]
        start = jnp.where(inside, jnp.where(lane == first + sub, 1.0, 0.0), here)
        solved = solve_eight(pivot, [row_splat(start, i) for i in range(8)])
        for step in range(1, groups):
            i = (g + step) % groups
            terms = [lane_splat(rows[i], first + j) * solved[j] for j in range(8)]
            while len(terms) > 1:
                terms = [terms[2 * q] + terms[2 * q + 1] for q in range(len(terms) // 2)]
            rows[i] = jnp.where(inside, 0.0, rows[i]) - terms[0]
        merged = solved[0]
        for j in range(1, 8):
            merged = jnp.where(sub == j, solved[j], merged)
        rows[g] = merged
    return rows


def three_parts(value):
    high = value.astype(BF16)
    rest = value - high.astype(F32)
    middle = rest.astype(BF16)
    return high, middle, (rest - middle.astype(F32)).astype(BF16)


def left_parts(value):
    high, middle, low = three_parts(value)
    return jnp.concatenate([high, high, middle, high, low, middle], axis=1)


def right_parts(value):
    high, middle, low = three_parts(value)
    return jnp.concatenate([high, middle, high, low, high, middle], axis=0)


def product(left, right):
    return jnp.dot(left, right, preferred_element_type=F32)


def eliminate(first, last, out_ref, left_ref, right_ref, diagonal_ref):
    order = out_ref.shape[0]
    blocks = order // TILE
    unit = lax.broadcasted_iota(jnp.int32, (TILE, TILE), 0) == lax.broadcasted_iota(
        jnp.int32, (TILE, TILE), 1
    )
    unit = jnp.where(unit, 1.0, 0.0)
    start = slice(TILE * first, TILE * first + TILE)
    diagonal_ref[...] = out_ref[start, start]
    left_ref[...] = jnp.zeros(left_ref.shape, BF16)
    right_ref[...] = jnp.zeros(right_ref.shape, BF16)

    def apply_last():
        wide = 2 * TILE
        for c in range(order // wide):
            here = slice(wide * c, wide * c + wide)
            out_ref[:, here] = out_ref[:, here] - product(left_ref[...], right_ref[:, here])

    def step(k, carry):
        here = pl.ds(pl.multiple_of(k * TILE, TILE), TILE)
        apply_last()
        block = diagonal_ref[...]
        rows = invert_tile([block[8 * i : 8 * i + 8, :] for i in range(TILE // 8)])
        inverse = jnp.concatenate(rows, axis=0)
        row = out_ref[here, :]
        out_ref[here, here] = -unit
        column = out_ref[:, here]
        out_ref[:, here] = jnp.zeros((order, TILE), F32)
        left_ref[...] = left_parts(product(left_parts(column), right_parts(inverse)))
        right_ref[...] = right_parts(row)
        right_ref[:, here] = right_parts(unit)
        out_ref[here, :] = jnp.zeros((TILE, order), F32)
        after = pl.ds(pl.multiple_of(jnp.minimum(k + 1, blocks - 1) * TILE, TILE), TILE)
        diagonal_ref[...] = out_ref[after, after] - product(left_ref[after, :], right_ref[:, after])
        return carry

    lax.fori_loop(first, last, step, 0)
    apply_last()


def inverse_kernel(slot_ref, own_ref, other_ref, out_ref, left_ref, right_ref, diagonal_ref):
    pairs, band, order = own_ref.shape
    for i in range(pairs):
        out_ref[pl.ds(pl.multiple_of(slot_ref[0, i] * band, 8), band), :] = own_ref[i]
        out_ref[pl.ds(pl.multiple_of(slot_ref[1, i] * band, 8), band), :] = other_ref[i]
    eliminate(0, order // TILE, out_ref, left_ref, right_ref, diagonal_ref)


def pivot_inverse(slots, own, other):
    order = own.shape[2]
    vmem = pl.BlockSpec(memory_space=pltpu.VMEM)
    return pl.pallas_call(
        inverse_kernel,
        out_shape=jax.ShapeDtypeStruct((order, order), F32),
        in_specs=[pl.BlockSpec(memory_space=pltpu.SMEM), vmem, vmem],
        out_specs=vmem,
        scratch_shapes=[
            pltpu.VMEM((order, 6 * TILE), BF16),
            pltpu.VMEM((6 * TILE, order), BF16),
            pltpu.VMEM((TILE, TILE), F32),
        ],
        compiler_params=pltpu.CompilerParams(vmem_limit_bytes=20 * 1024 * 1024),
        cost_estimate=pl.CostEstimate(flops=1, bytes_accessed=8, transcendentals=0),
        name="pivot_inverse",
    )(slots, own, other)


def iota(shape, axis):
    return lax.broadcasted_iota(jnp.int32, shape, axis)


def start_loads(sources, targets, sems):
    loads = [
        pltpu.make_async_copy(source, target, sems.at[i])
        for i, (source, target) in enumerate(zip(sources, targets))
    ]
    for load in loads:
        load.start()
    return loads


def scale_kernel(place_ref, inverse_hbm, column_hbm, out_ref, inverse_ref, column_ref, sems, *, band):
    loads = start_loads((inverse_hbm, column_hbm), (inverse_ref, column_ref), sems)
    shape = column_ref.shape
    loads[0].wait()
    right = right_parts(inverse_ref[...])
    pick = jnp.where(iota(shape, 0) == iota(shape, 1) + place_ref[0] * band, -1.0, 0.0)
    loads[1].wait()
    column = jnp.where(iota(shape, 1) < band, pick, column_ref[...])
    out_ref[...] = product(left_parts(column.T), right)


def update_kernel(
    place_ref, row_hbm, scaled_hbm, current_hbm, out_ref,
    row_ref, scaled_ref, current_ref, sems, *, band,
):
    loads = start_loads(
        (row_hbm, scaled_hbm, current_hbm), (row_ref, scaled_ref, current_ref), sems
    )
    rows, cols = current_ref.shape
    order = row_ref.shape[0]
    span = rows
    my_cols = place_ref[1] * (cols // span) * band

    def strip_of(shape):
        at = iota(shape, 1)
        inside = at < band
        within = at
        for g in range(1, cols // span):
            past = at - g * span
            now = (past >= 0) & (past < band)
            inside = inside | now
            within = jnp.where(now, past + g * band, within)
        return inside, within

    shape = (order, cols)
    inside, within = strip_of(shape)
    pick = jnp.where(iota(shape, 0) == within + my_cols, -1.0, 0.0)
    loads[0].wait()
    row_high, row_low, _ = three_parts(jnp.where(inside, pick, row_ref[...]))
    loads[1].wait()
    scaled_high, scaled_low, _ = three_parts(scaled_ref[...])
    change = product(
        jnp.concatenate([scaled_high, scaled_high, scaled_low], axis=1),
        jnp.concatenate([row_high, row_low, row_high], axis=0),
    )
    shape = (rows, cols)
    inside, _ = strip_of(shape)
    loads[2].wait()
    base = jnp.where(inside | (iota(shape, 0) < band), 0.0, current_ref[...])
    out_ref[...] = base - change


def loading_call(kernel, out_shape, flops, name, place, band, *arrays):
    return pl.pallas_call(
        functools.partial(kernel, band=band),
        out_shape=jax.ShapeDtypeStruct(out_shape, F32),
        in_specs=[pl.BlockSpec(memory_space=pltpu.SMEM)]
        + [pl.BlockSpec(memory_space=pl.ANY)] * len(arrays),
        out_specs=pl.BlockSpec(memory_space=pltpu.VMEM),
        scratch_shapes=[pltpu.VMEM(array.shape, F32) for array in arrays]
        + [pltpu.SemaphoreType.DMA((len(arrays),))],
        compiler_params=pltpu.CompilerParams(vmem_limit_bytes=56 * 1024 * 1024),
        cost_estimate=pl.CostEstimate(flops=flops, bytes_accessed=8, transcendentals=0),
        name=name,
    )(place, *arrays)


def body(matrix):
    rows, cols = matrix.shape
    groups = cols // rows
    depth = lax.axis_size("z")
    chips = lax.axis_size("x") * lax.axis_size("y")
    band = K * B // (2 * chips)
    core = lax.axis_index("c")
    place = jnp.stack([lax.axis_index(("x", "y", "c")), lax.axis_index("z")]).astype(jnp.int32)
    strip = jnp.concatenate(
        [matrix[:, g * rows : g * rows + band] for g in range(groups)], axis=1
    )
    rowband = matrix[0:band, :]
    with jax.named_scope("pivot_z"):
        padded = jnp.pad(strip[0:band, :], ((0, 0), (0, TILE - groups * band)))
        pivot = lax.all_to_all(jnp.broadcast_to(padded, (depth, band, TILE)), "z", 0, 0)
    pivot = pivot[:, :, : groups * band].transpose(1, 0, 2).reshape(band, K * B)
    with jax.named_scope("pivot_xy"):
        own = lax.all_to_all(jnp.broadcast_to(pivot, (chips, band, K * B)), ("x", "y"), 0, 0)
    spread = jnp.broadcast_to(rowband, (2 * chips, band, cols))
    turned, spread = lax.optimization_barrier((strip.T, spread))
    with jax.named_scope("column_panel"):
        column = lax.all_gather(turned, "z", axis=0, tiled=True)
    spread, own = lax.optimization_barrier((spread, own))
    with jax.named_scope("pivot_core"):
        other = lax.ppermute(own, "c", [(0, 1), (1, 0)])
    with jax.named_scope("row_panel"):
        row = lax.all_to_all(spread, ("x", "y", "c"), 0, 0)
    first = 2 * jnp.arange(chips, dtype=jnp.int32)
    slots = jnp.stack([first + core, first + 1 - core])
    order = K * B
    inverse = pivot_inverse(slots, own, other)
    scaled = loading_call(
        scale_kernel, (rows, order), 24*10**9, "scale", place, band, inverse, column
    )
    row = row.reshape(order, cols)
    return loading_call(
        update_kernel, (rows, cols), 1, "trailing_update", place, band, row, scaled, matrix
    )


def solution(mesh):
    split = Mesh(mesh.devices.reshape(4, 4, 2, 16), ("x", "y", "c", "z"))
    spec = P(("x", "y", "c"), "z")
    return jax.shard_map(body, mesh=split, in_specs=(spec,), out_specs=spec, check_vma=False)
```

```python
import functools

import jax
import jax.numpy as jnp
from jax import lax
from jax.experimental import pallas as pl
from jax.experimental.pallas import tpu as pltpu
from jax.sharding import Mesh
from jax.sharding import PartitionSpec as P

B = 384
K = 2
F32 = jnp.float32
BF16 = jnp.bfloat16
HIGHEST = lax.Precision.HIGHEST
TILE = 128


def lane_splat(tile, lane):
    return jnp.broadcast_to(tile[:, lane : lane + 1], (8, TILE))


def row_splat(tile, row):
    return jnp.broadcast_to(tile[row : row + 1, :], (8, TILE))


def solve_eight(pivot, right):
    size = 8
    pivot = [list(row) for row in pivot]
    right = list(right)
    factor = [[None] * size for _ in range(size)]
    scale = [None] * size
    for j in range(size):
        recip = 1.0 / pivot[j][j]
        scale[j] = recip
        for m in range(j + 1, size):
            factor[m][j] = pivot[m][j] * recip
        for m in range(j + 1, size):
            for q in range(j + 1, m + 1):
                pivot[m][q] = pivot[m][q] - (pivot[m][j] * pivot[q][j]) * recip
            right[m] = right[m] - factor[m][j] * right[j]
    for j in range(size):
        right[j] = right[j] * scale[j]
    for j in reversed(range(size)):
        for m in range(j):
            right[m] = right[m] - factor[j][m] * right[j]
    return right


def invert_tile(rows):
    lane = lax.broadcasted_iota(jnp.int32, (8, TILE), 1)
    sub = lax.broadcasted_iota(jnp.int32, (8, TILE), 0)
    groups = len(rows)
    rows = list(rows)
    for g in range(groups):
        first = 8 * g
        here = rows[g]
        inside = (lane >= first) & (lane < first + 8)
        columns = [lane_splat(here, first + j) for j in range(8)]
        pivot = [[row_splat(columns[j], i) for j in range(i + 1)] for i in range(8)]
        start = jnp.where(inside, jnp.where(lane == first + sub, 1.0, 0.0), here)
        solved = solve_eight(pivot, [row_splat(start, i) for i in range(8)])
        for step in range(1, groups):
            i = (g + step) % groups
            terms = [lane_splat(rows[i], first + j) * solved[j] for j in range(8)]
            while len(terms) > 1:
                terms = [terms[2 * q] + terms[2 * q + 1] for q in range(len(terms) // 2)]
            rows[i] = jnp.where(inside, 0.0, rows[i]) - terms[0]
        merged = solved[0]
        for j in range(1, 8):
            merged = jnp.where(sub == j, solved[j], merged)
        rows[g] = merged
    return rows


def three_parts(value):
    high = value.astype(BF16)
    rest = value - high.astype(F32)
    middle = rest.astype(BF16)
    return high, middle, (rest - middle.astype(F32)).astype(BF16)


def left_parts(value):
    high, middle, low = three_parts(value)
    return jnp.concatenate([high, high, middle, high, low, middle], axis=1)


def right_parts(value):
    high, middle, low = three_parts(value)
    return jnp.concatenate([high, middle, high, low, high, middle], axis=0)


def product(left, right):
    return jnp.dot(left, right, preferred_element_type=F32)


def eliminate(first, last, out_ref, left_ref, right_ref, diagonal_ref):
    order = out_ref.shape[0]
    blocks = order // TILE
    unit = lax.broadcasted_iota(jnp.int32, (TILE, TILE), 0) == lax.broadcasted_iota(
        jnp.int32, (TILE, TILE), 1
    )
    unit = jnp.where(unit, 1.0, 0.0)
    start = slice(TILE * first, TILE * first + TILE)
    diagonal_ref[...] = out_ref[start, start]

    def apply_last():
        wide = 2 * TILE
        for c in range(order // wide):
            here = slice(wide * c, wide * c + wide)
            out_ref[:, here] = out_ref[:, here] - product(left_ref[...], right_ref[:, here])

    def step(k, carry, pending=True):
        here = pl.ds(pl.multiple_of(k * TILE, TILE), TILE)
        if pending:
            apply_last()
        block = diagonal_ref[...]
        rows = invert_tile([block[8 * i : 8 * i + 8, :] for i in range(TILE // 8)])
        inverse = jnp.concatenate(rows, axis=0)
        row = out_ref[here, :]
        out_ref[here, here] = -unit
        column = out_ref[:, here]
        out_ref[:, here] = jnp.zeros((order, TILE), F32)
        left_ref[...] = left_parts(product(left_parts(column), right_parts(inverse)))
        right_ref[...] = right_parts(row)
        right_ref[:, here] = right_parts(unit)
        out_ref[here, :] = jnp.zeros((TILE, order), F32)
        after = pl.ds(pl.multiple_of(jnp.minimum(k + 1, blocks - 1) * TILE, TILE), TILE)
        diagonal_ref[...] = out_ref[after, after] - product(left_ref[after, :], right_ref[:, after])
        return carry

    step(jnp.int32(first), 0, pending=False)
    lax.fori_loop(first + 1, last, step, 0)
    apply_last()


def inverse_kernel(slot_ref, own_ref, other_ref, out_ref, left_ref, right_ref, diagonal_ref):
    pairs, band, order = own_ref.shape
    for i in range(pairs):
        out_ref[pl.ds(pl.multiple_of(slot_ref[0, i] * band, 8), band), :] = own_ref[i]
        out_ref[pl.ds(pl.multiple_of(slot_ref[1, i] * band, 8), band), :] = other_ref[i]
    eliminate(0, order // TILE, out_ref, left_ref, right_ref, diagonal_ref)


def pivot_inverse(slots, own, other):
    order = own.shape[2]
    vmem = pl.BlockSpec(memory_space=pltpu.VMEM)
    return pl.pallas_call(
        inverse_kernel,
        out_shape=jax.ShapeDtypeStruct((order, order), F32),
        in_specs=[pl.BlockSpec(memory_space=pltpu.SMEM), vmem, vmem],
        out_specs=vmem,
        scratch_shapes=[
            pltpu.VMEM((order, 6 * TILE), BF16),
            pltpu.VMEM((6 * TILE, order), BF16),
            pltpu.VMEM((TILE, TILE), F32),
        ],
        compiler_params=pltpu.CompilerParams(vmem_limit_bytes=20 * 1024 * 1024),
        cost_estimate=pl.CostEstimate(flops=1, bytes_accessed=8, transcendentals=0),
        name="pivot_inverse",
    )(slots, own, other)


def iota(shape, axis):
    return lax.broadcasted_iota(jnp.int32, shape, axis)


def start_loads(sources, targets, sems):
    loads = [
        pltpu.make_async_copy(source, target, sems.at[i])
        for i, (source, target) in enumerate(zip(sources, targets))
    ]
    for load in loads:
        load.start()
    return loads


def scale_kernel(place_ref, inverse_hbm, column_hbm, out_ref, inverse_ref, column_ref, sems, *, band):
    loads = start_loads((inverse_hbm, column_hbm), (inverse_ref, column_ref), sems)
    shape = column_ref.shape
    loads[0].wait()
    right = right_parts(inverse_ref[...])
    pick = jnp.where(iota(shape, 0) == iota(shape, 1) + place_ref[0] * band, -1.0, 0.0)
    loads[1].wait()
    column = jnp.where(iota(shape, 1) < band, pick, column_ref[...])
    out_ref[...] = product(left_parts(column.T), right)


def update_kernel(
    place_ref, row_hbm, scaled_hbm, current_hbm, out_ref,
    row_ref, scaled_ref, current_ref, sems, *, band,
):
    loads = start_loads(
        (row_hbm, scaled_hbm, current_hbm), (row_ref, scaled_ref, current_ref), sems
    )
    rows, cols = current_ref.shape
    order = row_ref.shape[0]
    span = rows
    my_cols = place_ref[1] * (cols // span) * band

    def strip_of(shape):
        at = iota(shape, 1)
        inside = at < band
        within = at
        for g in range(1, cols // span):
            past = at - g * span
            now = (past >= 0) & (past < band)
            inside = inside | now
            within = jnp.where(now, past + g * band, within)
        return inside, within

    shape = (order, cols)
    inside, within = strip_of(shape)
    pick = jnp.where(iota(shape, 0) == within + my_cols, -1.0, 0.0)
    loads[0].wait()
    row_high, row_low, _ = three_parts(jnp.where(inside, pick, row_ref[...]))
    loads[1].wait()
    scaled_high, scaled_low, _ = three_parts(scaled_ref[...])
    change = product(
        jnp.concatenate([scaled_high, scaled_high, scaled_low], axis=1),
        jnp.concatenate([row_high, row_low, row_high], axis=0),
    )
    shape = (rows, cols)
    inside, _ = strip_of(shape)
    loads[2].wait()
    base = jnp.where(inside | (iota(shape, 0) < band), 0.0, current_ref[...])
    out_ref[...] = base - change


def loading_call(kernel, out_shape, flops, name, place, band, *arrays):
    return pl.pallas_call(
        functools.partial(kernel, band=band),
        out_shape=jax.ShapeDtypeStruct(out_shape, F32),
        in_specs=[pl.BlockSpec(memory_space=pltpu.SMEM)]
        + [pl.BlockSpec(memory_space=pl.ANY)] * len(arrays),
        out_specs=pl.BlockSpec(memory_space=pltpu.VMEM),
        scratch_shapes=[pltpu.VMEM(array.shape, F32) for array in arrays]
        + [pltpu.SemaphoreType.DMA((len(arrays),))],
        compiler_params=pltpu.CompilerParams(vmem_limit_bytes=52 * 1024 * 1024),
        cost_estimate=pl.CostEstimate(flops=flops, bytes_accessed=8, transcendentals=0),
        name=name,
    )(place, *arrays)


def body(matrix):
    rows, cols = matrix.shape
    groups = cols // rows
    depth = lax.axis_size("z")
    chips = lax.axis_size("x") * lax.axis_size("y")
    band = K * B // (2 * chips)
    core = lax.axis_index("c")
    place = jnp.stack([lax.axis_index(("x", "y", "c")), lax.axis_index("z")]).astype(jnp.int32)
    strip = jnp.concatenate(
        [matrix[:, g * rows : g * rows + band] for g in range(groups)], axis=1
    )
    rowband = matrix[0:band, :]
    with jax.named_scope("pivot_z"):
        padded = jnp.pad(strip[0:band, :], ((0, 0), (0, TILE - groups * band)))
        pivot = lax.all_to_all(jnp.broadcast_to(padded, (depth, band, TILE)), "z", 0, 0)
    pivot = pivot[:, :, : groups * band].transpose(1, 0, 2).reshape(band, K * B)
    with jax.named_scope("pivot_xy"):
        own = lax.all_to_all(jnp.broadcast_to(pivot, (chips, band, K * B)), ("x", "y"), 0, 0)
    spread = jnp.broadcast_to(rowband, (2 * chips, band, cols))
    turned, spread = lax.optimization_barrier((strip.T, spread))
    with jax.named_scope("column_panel"):
        column = lax.all_gather(turned, "z", axis=0, tiled=True)
    spread, own = lax.optimization_barrier((spread, own))
    with jax.named_scope("pivot_core"):
        other = lax.ppermute(own, "c", [(0, 1), (1, 0)])
    with jax.named_scope("row_panel"):
        row = lax.all_to_all(spread, ("x", "y", "c"), 0, 0)
    first = 2 * jnp.arange(chips, dtype=jnp.int32)
    slots = jnp.stack([first + core, first + 1 - core])
    order = K * B
    inverse = pivot_inverse(slots, own, other)
    scaled = loading_call(
        scale_kernel, (rows, order), 24*10**9, "scale", place, band, inverse, column
    )
    row = row.reshape(order, cols)
    return loading_call(
        update_kernel, (rows, cols), 1, "trailing_update", place, band, row, scaled, matrix
    )


def solution(mesh):
    split = Mesh(mesh.devices.reshape(4, 4, 2, 16), ("x", "y", "c", "z"))
    spec = P(("x", "y", "c"), "z")
    return jax.shard_map(body, mesh=split, in_specs=(spec,), out_specs=spec, check_vma=False)
```
